128 devices in a mesh: sub: 16 (over x, z), crs: 8 (over y, core).
Axes of the slice: x: 4, y: 4, z: 4, core: 2. Of those that a mesh axis runs over, the one named last changes fastest.
Arguments:
- right_side: float32 [64, 2097152], P(None, ('sub', 'crs')), may hold values from -18 to 18
- kappa_sq: float32 [2097152], P(('sub', 'crs')), may hold values from 0.05 to 0.5
- conduct: float32 [2097152], P(('sub', 'crs')), may hold values from 0.1 to 1
- partners: int32 [16384, 4], P(('sub', 'crs')), may hold values from 0 to 16383, as said below
- local_factor: float32 [16384, 128, 128], P(('sub', 'crs')), may hold values from -1 to 3
- restrict_weight: float32 [2097152], P(('sub', 'crs')), may hold values from 0.1 to 0.5
- aggregate: int32 [128, 16384], P(('sub', 'crs')), may hold values from 0 to 511, never falling along the last dimension, each value on 1 to 64 neighbouring positions
- owner: int32 [65536, 1], P(('sub', 'crs')), may hold values from 0 to 15; in each aligned block of 512 rows (0 to 511, 512 to 1023, ...) at most 128 rows name the same one
- owner_coarse_row: int32 [65536], P(('sub', 'crs')), may hold values from 0 to 511
- coarse_factor: float32 [8192, 8192], P('crs', 'sub'), may hold values from -0.0625 to 0.0625
Outputs:
- solution: float32 [64, 2097152], P(None, ('sub', 'crs'))
- residual: float32 [64, 2097152], P(None, ('sub', 'crs'))
The draws below stay inside these ranges and needn't reach their ends.
Inputs may be any that keep to these rules, and one draw needn't show every extreme that they name: In every slot k the relation is mutual: partners[partners[b, k], k] = b; a block may name itself; every partner lies on its block's subdomain or at most 7 blocks beyond its edge, and slot 0 stays on the subdomain. `aggregate`: each subdomain's row numbers its 512 slots in node order; every slot holds 1 to 64 nodes, and some slot holds exactly 64. Among the 512 slots of one subdomain no owner group is named more than 128 times, a bound that some block reaches.
All inputs are finite; a program needn't handle non-finite values.
Results may differ from the reference program's by a relative error of at most 0.0001.
Values sent between devices are 32-bit elements; how exact they have to be, the bound alone decides.
A program may use at most 256 MiB of HBM per device.

```python
import math
import jax
import jax.numpy as jnp
import numpy as np
from jax import lax

BS = 128
SMP = 64
NC = 8192
ITERS = 2
NODE_DEV = 16384
NODES = 2097152
NBLOCKS = 16384
SUBDOMAIN_SLOTS = 512
TOTAL_SLOTS = 65536
GROUP_COARSE_ROWS = 512
OWNER_SLOT_LIMIT = 128
N_SUB = 16
N_CRS = 8


def draw_right_side(key, part):
    spread = jnp.arange(NODES, dtype=jnp.float32) / NODES
    values = jax.random.truncated_normal(key, -6.0, 6.0, (SMP, NODES), jnp.float32)
    factor = 1.0 + 2.0 * spread
    return (values * factor[None, :]).astype(jnp.float32)


def draw_partners(key, part):
    blocks_all = jnp.arange(NBLOCKS, dtype=jnp.int32)
    window_count = NBLOCKS // 8 + 2
    columns = []
    for slot_index, offset in enumerate((0, 1, 4, 7)):
        window_keys = jax.random.split(jax.random.fold_in(key, 17 + slot_index), window_count)
        orders = jax.vmap(lambda single: jax.random.permutation(single, 8))(window_keys).astype(jnp.int32)
        order_ranks = jnp.argsort(orders, axis=1).astype(jnp.int32)
        shifted = blocks_all - offset + 8
        window = shifted // 8
        position = shifted % 8
        mate_rank = jnp.bitwise_xor(order_ranks[window, position], 1)
        partner = blocks_all - position + orders[window, mate_rank]
        inside = jnp.logical_and(partner >= 0, partner < NBLOCKS)
        columns.append(jnp.where(inside, partner, blocks_all))
    return jnp.stack(columns, axis=1).astype(jnp.int32)


def draw_local_factor(key, part):
    first_key, second_key = jax.random.split(key)
    identity = jnp.eye(BS, dtype=jnp.float32)
    spread_off = jax.random.uniform(first_key, (NBLOCKS, BS, BS), jnp.float32, -1.0, 1.0) * (0.5 / math.sqrt(BS))
    diagonal = jax.random.uniform(second_key, (NBLOCKS, BS), jnp.float32, 1.0, 2.0)
    return (spread_off * (1.0 - identity) + diagonal[:, :, None] * identity).astype(jnp.float32)


def with_ends(array, key, least, high):
    longest = array.shape.index(max(array.shape))
    spots = []
    for shift in (0, 1):
        where = [jax.random.randint(jax.random.fold_in(key, axis), (), 0, length) for axis, length in enumerate(array.shape)]
        where[longest] = (where[longest] + shift) % array.shape[longest]
        spots.append(tuple(where))
    return array.at[spots[0]].set(least).at[spots[1]].set(high)


def block_levels(own_key, shape, pieces, low, high):
    def one(dim, shards_of):
        heights = jax.random.uniform(jax.random.fold_in(jax.random.fold_in(own_key, 6), dim), (shards_of,), jnp.float32, low / len(pieces), high / len(pieces))
        return jnp.repeat(jnp.exp(heights), shape[dim] // shards_of).reshape((-1,) + (1,) * (len(shape) - dim - 1))

    factor_of = one(*pieces[0])
    for cut in pieces[1:]:
        factor_of = factor_of * one(*cut)
    return factor_of


def split_up(number_of, total, most, skew):
    loads = [(1 << 20) // math.isqrt(standing ** skew) + 1 for standing in range(2, number_of + 1)]
    surplus, counts = total - most - (number_of - 1), [1] * (number_of - 1)
    while surplus > 0:
        free = [i for i in range(number_of - 1) if counts[i] < most]
        pool, budget = sum([loads[i] for i in free]), surplus
        for i in free:
            more = min(most - counts[i], max(1, budget * loads[i] // pool), surplus)
            counts[i] = counts[i] + more
            surplus = surplus - more
    return np.array([most] + counts)


def uneven_parts(stream_key, count, total, limit, skew):
    if count == 2:
        one = jax.random.randint(stream_key, (), max(1, total - limit), min(limit, total - 1) + 1)
        return jnp.stack([one, total - one])
    lengths = jnp.asarray(split_up(count, total, limit, skew), jnp.int32)
    twos = (count - 1) // 2
    source_of, taker = lengths[1:1 + 2 * twos:2], lengths[2:2 + 2 * twos:2]
    margin = jnp.minimum(source_of - 1, limit - taker)
    passed = jax.random.randint(jax.random.fold_in(stream_key, 1), (twos,), 0, 1 << 20) % (margin + 1)
    lengths = lengths.at[1:1 + 2 * twos:2].set(source_of - passed).at[2:2 + 2 * twos:2].set(taker + passed)
    return lengths[jax.random.permutation(jax.random.fold_in(stream_key, 2), count)]


def deal_out(key, own, number, rows, count, top, reach, slope):
    ranking = jax.random.permutation(key, count)
    packed, common = shares(count, rows * top, reach, slope, True), shares(count, rows * top, reach, slope, False)
    places = jnp.arange(count)

    def named(sizes, rotation):
        used = int((sizes > 0).sum())
        fixed = max(1, used // 4)
        moved = fixed + (places - fixed + rotation * (used - fixed)) % max(1, count - fixed)
        return jnp.zeros((count,), jnp.int32).at[ranking[jnp.where(places < fixed, places, moved)]].set(jnp.asarray(sizes, jnp.int32))

    sizes = jnp.where(number % 4 == 0, named(packed, number // 4), named(common, number - number // 4 - 1))
    mixed = jax.random.permutation(jax.random.fold_in(own, 3), count)
    giver, receiver = mixed[0:count // 2 * 2:2], mixed[1:count // 2 * 2:2]
    slack = jnp.minimum(sizes[giver] - 1, reach - sizes[receiver]) // 2
    slack = jnp.where((giver == ranking[0]) | (receiver == ranking[0]) | (sizes[receiver] == 0), 0, jnp.maximum(slack, 0))
    moved = jax.random.randint(jax.random.fold_in(own, 4), (count // 2,), 0, 1 << 20) % (slack + 1)
    sizes = sizes.at[giver].add(-moved).at[receiver].add(moved)
    labels = jnp.searchsorted(jnp.cumsum(sizes), jnp.arange(rows * top), side="right").astype(jnp.int32)
    table = labels.reshape(top, rows).T
    table = table[jax.random.permutation(jax.random.fold_in(own, 1), rows)]
    rotation = jax.random.randint(jax.random.fold_in(own, 2), (rows, 1), 0, top)
    return jnp.take_along_axis(table, (jnp.arange(top)[None, :] + rotation) % top, axis=1)


def shares(number_of, total, reach, slope, full):
    portions = [(1 << 20) // math.isqrt(rank ** slope) + 1 for rank in range(1, number_of + 1)]
    largest = reach if full else min(reach, max(-(-total // number_of), total * portions[0] // sum(portions)))
    least = 1 if total - largest >= number_of - 1 else 0
    given, rest = [largest] + [least] * (number_of - 1), total - largest - least * (number_of - 1)
    while rest > 0:
        free = [i for i in range(1, number_of) if given[i] < largest] or [i for i in range(1, number_of) if given[i] < reach]
        mass, left = sum([portions[i] for i in free]), rest
        for i in free:
            addition = min(reach - given[i], max(1, left * portions[i] // mass), rest)
            given[i] = given[i] + addition
            rest = rest - addition
    return np.array(given)


def centred(rng, extent, width, most, pieces=(), kind=jnp.bfloat16):
    loudness = block_levels(rng, extent, pieces, -0.22, 0.18) if pieces else 1.0
    entries = jax.random.normal(rng, extent, jnp.float32) * width * loudness
    return jnp.minimum(jnp.maximum(entries, -most), most).astype(kind)


def setup_inputs(seed: int = 0) -> dict:
    key_of = jax.random.split(jax.random.key(seed), 11)
    right_side = draw_right_side(jax.random.fold_in(key_of[10], 71), 0)
    kappa_sq = jnp.clip(jnp.exp(math.log(0.5) - 2.3025851 * jax.random.uniform(key_of[1], (NODES,), jnp.float32) ** block_levels(key_of[1], (NODES,), ((0, 128),), -0.2, 0.2)), 0.05, 0.5)
    conduct = jnp.clip(jnp.exp(math.log(1.0) - 2.3025851 * jax.random.uniform(key_of[2], (NODES,), jnp.float32) ** block_levels(key_of[2], (NODES,), ((0, 128),), -0.2, 0.2)), 0.1, 1.0)
    partners = draw_partners(jax.random.fold_in(key_of[10], 71), 0)
    local_factor = draw_local_factor(jax.random.fold_in(key_of[10], 71), 0)
    restrict_weight = jnp.clip(jnp.exp(math.log(0.5) - 1.609438 * jax.random.uniform(key_of[5], (NODES,), jnp.float32) ** block_levels(key_of[5], (NODES,), ((0, 128),), -0.2, 0.2)), 0.1, 0.5)
    aggregate = jax.vmap(lambda own: jnp.searchsorted(jnp.cumsum(uneven_parts(own, SUBDOMAIN_SLOTS, NODE_DEV, 64, 1)), jnp.arange(NODE_DEV), side="right"))(jax.random.split(key_of[6], (N_SUB * N_CRS))).reshape((N_SUB * N_CRS, NODE_DEV)).astype(jnp.int32)
    owner_keys = jax.random.split(jax.random.fold_in(key_of[7], 1), TOTAL_SLOTS // SUBDOMAIN_SLOTS)
    owner_turns = jax.random.permutation(jax.random.fold_in(key_of[7], 3), TOTAL_SLOTS // SUBDOMAIN_SLOTS)
    owner = jax.vmap(lambda own, number: deal_out(jax.random.fold_in(key_of[7], 2), own, number, SUBDOMAIN_SLOTS, N_SUB, 1, OWNER_SLOT_LIMIT, 2))(owner_keys, owner_turns).reshape((TOTAL_SLOTS, 1))
    owner_coarse_row = with_ends(jax.random.randint(key_of[8], (TOTAL_SLOTS,), 0, GROUP_COARSE_ROWS), jax.random.fold_in(key_of[8], 1), 0, GROUP_COARSE_ROWS - 1).astype(jnp.int32)
    coarse_factor = centred(key_of[9], (NC, NC), NC ** -0.5, 0.0625, ((0, 8), (1, 16)), jnp.float32)
    return {"right_side": right_side, "kappa_sq": kappa_sq, "conduct": conduct, "partners": partners, "local_factor": local_factor, "restrict_weight": restrict_weight, "aggregate": aggregate, "owner": owner, "owner_coarse_row": owner_coarse_row, "coarse_factor": coarse_factor}


def reference(right_side, kappa_sq, conduct, partners, local_factor, restrict_weight, aggregate, owner, owner_coarse_row, coarse_factor):
    block_count = partners.shape[0]
    highest = lax.Precision.HIGHEST
    conduct_blocks = conduct.reshape(block_count, BS)
    kappa_blocks = kappa_sq.reshape(block_count, BS)
    partner_wt = [0.5 * (conduct_blocks + conduct_blocks[partners[:, k]]) for k in range(4)]
    chain_weight = 0.5 * (conduct_blocks[:, :-1] + conduct_blocks[:, 1:])

    def apply_precision(vector_in):
        blocks = vector_in.reshape(SMP, block_count, BS)
        result = kappa_blocks * blocks
        for k in range(4):
            partner_vals = jnp.take(blocks, partners[:, k], axis=1)
            result = result + partner_wt[k] * (blocks - partner_vals)
        chain_flux = chain_weight * (blocks[:, :, :-1] - blocks[:, :, 1:])
        result = result + jnp.pad(chain_flux, ((0, 0), (0, 0), (0, 1))) - jnp.pad(chain_flux, ((0, 0), (0, 0), (1, 0)))
        return result.reshape(SMP, NODES)

    device_ids = jnp.arange(N_SUB * N_CRS, dtype=jnp.int32)
    node_slot_table = (device_ids[:, None] * SUBDOMAIN_SLOTS + aggregate).reshape(-1).astype(jnp.int32)
    coarse_ids = (owner[:, 0] * (NC // N_SUB) + owner_coarse_row).astype(jnp.int32)

    def coarse_level(vector_in):
        weighted_values = vector_in * restrict_weight[None, :]
        restriction_tiles = jax.ops.segment_sum(weighted_values.T, node_slot_table, num_segments=TOTAL_SLOTS, indices_are_sorted=True).T
        coarse_vec = jnp.zeros((SMP, NC), jnp.float32).at[:, coarse_ids].add(restriction_tiles)
        halfway = lax.dot_general(coarse_vec, coarse_factor, (((1,), (1,)), ((), ())), precision=highest)
        lifted = jnp.dot(halfway, coarse_factor, precision=highest)
        slot_values = jnp.take(lifted, coarse_ids, axis=1)
        return restrict_weight[None, :] * jnp.take(slot_values, node_slot_table, axis=1)

    def precondition(vector_in):
        blocks = vector_in.reshape(SMP, block_count, BS)
        halfway = jnp.einsum('sbn,bnm->sbm', blocks, local_factor, precision=highest)
        local_part = jnp.einsum('sbm,bnm->sbn', halfway, local_factor, precision=highest).reshape(SMP, NODES)
        return local_part + coarse_level(vector_in)

    solution = jnp.zeros_like(right_side)
    residual = right_side
    precond = precondition(residual)
    direction = precond
    norm_now = jnp.sum(residual * precond, axis=1)
    for step in range(ITERS):
        image = apply_precision(direction)
        step_size = norm_now / jnp.sum(direction * image, axis=1)
        solution = solution + step_size[:, None] * direction
        residual = residual - step_size[:, None] * image
        if step + 1 < ITERS:
            precond = precondition(residual)
            norm_next = jnp.sum(residual * precond, axis=1)
            direction = precond + (norm_next / norm_now)[:, None] * direction
            norm_now = norm_next
    return solution, residual
```

```python
import functools

import jax
import jax.numpy as jnp
from jax import lax
from jax.experimental import pallas as pl
from jax.experimental.pallas import tpu as pltpu
from jax.sharding import PartitionSpec as P

MESH = pl.DeviceIdType.MESH
F32 = jnp.float32
BF16 = jnp.bfloat16
HALO = 7
BS = 128
SMP = 64
LIMIT = 128


def split(x):
    high = x.astype(BF16)
    return high, (x - high.astype(F32)).astype(BF16)


def dot(a, b):
    return lax.dot_general(a, b, (((1,), (0,)), ((), ())), preferred_element_type=F32)


def dot_t(a, b):
    return lax.dot_general(a, b, (((1,), (1,)), ((), ())), preferred_element_type=F32)


def stacked(x):
    return jnp.concatenate(split(x), axis=0)


def folded(y):
    half = y.shape[0] // 2
    return y[:half] + y[half:]


def one_hot(mask):
    return jnp.where(mask, 1.0, 0.0).astype(BF16)


def apply_kernel(
    n_sub,
    n_crs,
    src_hbm,
    factor_hbm,
    coarse_hbm,
    weight_ref,
    kappa_ref,
    cond_ref,
    slot_ref,
    owner_ref,
    row_ref,
    partner_ref,
    z_hbm,
    q_hbm,
    dots_ref,
    src_v,
    factor_v,
    coarse_v,
    ext_v,
    cond_v,
    q_v,
    acc_v,
    place_v,
    scatter_v,
    index_send,
    index_recv,
    slot_send,
    slot_recv,
    back_send,
    back_recv,
    cpart,
    crecv,
    cfull,
    ipart,
    irecv,
    ifull,
    lpart,
    lrecv,
    lfull,
    slot_v,
    load_sem,
    store_sem,
    sub_send,
    sub_recv,
    crs_send,
    crs_recv,
    halo_send,
    halo_recv,
):
    sub = lax.axis_index("sub")
    crs = lax.axis_index("crs")
    me = sub * n_crs + crs
    total = n_sub * n_crs
    right = lax.rem(me + 1, total)
    left = lax.rem(me + total - 1, total)
    nodes = src_v.shape[1]
    blocks = nodes // BS
    slots = owner_ref.shape[1]
    halo = HALO * BS

    def sub_peer(j):
        return lax.rem(sub + j, n_sub)

    def sub_from(j):
        return lax.rem(sub + n_sub - j, n_sub)

    def crs_peer(j):
        return lax.rem(crs + j, n_crs)

    def crs_from(j):
        return lax.rem(crs + n_crs - j, n_crs)

    def at_device(d):
        return (d // n_crs, lax.rem(d, n_crs))

    def sub_copy(phase, j, source, target):
        return pltpu.make_async_remote_copy(
            src_ref=source,
            dst_ref=target,
            send_sem=sub_send.at[phase, j],
            recv_sem=sub_recv.at[phase, j],
            device_id=(sub_peer(j), crs),
            device_id_type=MESH,
        )

    def crs_copy(phase, j, source, target):
        return pltpu.make_async_remote_copy(
            src_ref=source,
            dst_ref=target,
            send_sem=crs_send.at[phase, j],
            recv_sem=crs_recv.at[phase, j],
            device_id=(sub, crs_peer(j)),
            device_id_type=MESH,
        )

    def lanes(ref, i):
        return ref.at[:, pl.ds(pl.multiple_of(i * LIMIT, LIMIT), LIMIT)]

    def start_all(count, copy):
        @pl.loop(1, count)
        def _(j):
            copy(j).start()

    def wait_all(count, copy):
        @pl.loop(1, count)
        def _(j):
            copy(j).wait()

    loads = [
        pltpu.make_async_copy(src_hbm, src_v, load_sem.at[0]),
        pltpu.make_async_copy(factor_hbm, factor_v, load_sem.at[1]),
        pltpu.make_async_copy(coarse_hbm, coarse_v, load_sem.at[2]),
    ]
    for load in loads:
        load.start()

    barrier = pltpu.get_barrier_semaphore()

    @pl.loop(1, n_sub)
    def _(j):
        pl.semaphore_signal(barrier, inc=1, device_id=(sub_peer(j), crs), device_id_type=MESH)

    @pl.loop(1, n_crs)
    def _(j):
        pl.semaphore_signal(barrier, inc=1, device_id=(sub, crs_peer(j)), device_id_type=MESH)

    pl.semaphore_signal(barrier, inc=1, device_id=at_device(left), device_id_type=MESH)
    pl.semaphore_signal(barrier, inc=1, device_id=at_device(right), device_id_type=MESH)

    owner_row = owner_ref[...]
    group = lax.broadcasted_iota(jnp.int32, (n_sub, slots), 0)
    members = jnp.where(owner_row == group, 1.0, 0.0)
    before = one_hot(
        lax.broadcasted_iota(jnp.int32, (slots, slots), 0)
        < lax.broadcasted_iota(jnp.int32, (slots, slots), 1)
    )
    ahead = dot(members.astype(BF16), before)
    rank = jnp.sum(members * ahead, axis=0, keepdims=True)
    place = owner_row * LIMIT + rank.astype(jnp.int32)
    row_one = stacked(jnp.broadcast_to((row_ref[...] + 1).astype(F32), (8, slots)))

    @pl.loop(0, n_sub)
    def _(i):
        start = pl.multiple_of(i * LIMIT, LIMIT)
        hot = one_hot(lax.broadcasted_iota(jnp.int32, (LIMIT, slots), 0) + start == place)
        place_v[pl.ds(start, LIMIT), :] = hot
        index_send[i] = folded(dot_t(row_one, hot)) - 1.0

    cond_v[:, pl.ds(halo, nodes)] = cond_ref[...]
    index_recv[sub] = index_send[sub]

    pl.semaphore_wait(barrier, n_sub + n_crs)

    def index_copy(j):
        return sub_copy(0, j, index_send.at[sub_peer(j)], index_recv.at[sub])

    def index_wait(j):
        return sub_copy(0, j, index_send.at[sub_peer(j)], index_recv.at[sub_from(j)])

    start_all(n_sub, index_copy)

    def halo_copies(buffer, phase):
        up = pltpu.make_async_remote_copy(
            src_ref=buffer.at[:, pl.ds(nodes, halo)],
            dst_ref=buffer.at[:, pl.ds(0, halo)],
            send_sem=halo_send.at[phase],
            recv_sem=halo_recv.at[phase],
            device_id=at_device(right),
            device_id_type=MESH,
        )
        down = pltpu.make_async_remote_copy(
            src_ref=buffer.at[:, pl.ds(halo, halo)],
            dst_ref=buffer.at[:, pl.ds(halo + nodes, halo)],
            send_sem=halo_send.at[phase + 1],
            recv_sem=halo_recv.at[phase + 1],
            device_id=at_device(left),
            device_id_type=MESH,
        )
        return up, down

    cond_copies = halo_copies(cond_v, 0)
    for copy in cond_copies:
        copy.start()

    loads[0].wait()
    chunk = 1024
    acc_v[...] = jnp.zeros_like(acc_v)

    @pl.loop(0, nodes // chunk)
    def _(i):
        span = pl.ds(pl.multiple_of(i * chunk, chunk), chunk)
        weighted = src_v[:, span] * weight_ref[:, span]
        hot = one_hot(lax.broadcasted_iota(jnp.int32, (slots, chunk), 0) == slot_ref[:, span])
        acc_v[...] += dot_t(stacked(weighted), hot)

    tiles = stacked(folded(acc_v[...]))
    for i in range(0, n_sub, 2):
        slot_send[:, i * LIMIT : (i + 2) * LIMIT] = folded(
            dot_t(tiles, place_v[i * LIMIT : (i + 2) * LIMIT, :])
        )

    def slot_copy(j):
        return sub_copy(1, j, lanes(slot_send, sub_peer(j)), lanes(slot_recv, sub))

    def slot_wait(j):
        return sub_copy(1, j, lanes(slot_send, sub_peer(j)), lanes(slot_recv, sub_from(j)))

    start_all(n_sub, slot_copy)
    own = pl.ds(pl.multiple_of(sub * LIMIT, LIMIT), LIMIT)
    slot_recv[:, own] = slot_send[:, own]

    def local(first, last):
        @pl.loop(first // 4, last // 4)
        def _(g):
            for k in range(4):
                b = g * 4 + k
                at = pl.multiple_of(b * BS, BS)
                values = stacked(src_v[:, pl.ds(at, BS)])
                high, low = split(factor_v[b])
                half = folded(dot(values, high)) + dot(values[:SMP], low)
                half = stacked(half)
                ext_v[:, pl.ds(pl.multiple_of(at + halo, BS), BS)] = folded(
                    dot_t(half, high)
                ) + dot_t(half[:SMP], low)

    loads[1].wait()
    local(0, 32)

    wait_all(n_sub, index_wait)

    @pl.loop(0, n_sub)
    def _(i):
        index = index_recv[i][0:1, :].astype(jnp.int32)
        rows = scatter_v.shape[0]
        span = pl.ds(pl.multiple_of(i * LIMIT, LIMIT), LIMIT)
        scatter_v[:, span] = one_hot(lax.broadcasted_iota(jnp.int32, (rows, LIMIT), 0) == index)

    wait_all(n_sub, slot_wait)
    coarse_part = folded(dot_t(stacked(slot_recv[...]), scatter_v[...]))
    cpart[...] = coarse_part.reshape(cpart.shape)

    def reduce_sub(phase, part, recv, full, gap):
        def out(j):
            return sub_copy(phase, j, part.at[sub_peer(j)], recv.at[sub])

        def come(j):
            return sub_copy(phase, j, part.at[sub_peer(j)], recv.at[sub_from(j)])

        def share(j):
            return sub_copy(phase + 1, j, full.at[sub], full.at[sub])

        def shared(j):
            return sub_copy(phase + 1, j, full.at[sub], full.at[sub_from(j)])

        start_all(n_sub, out)
        recv[sub] = part[sub]
        local(gap, gap + 16)
        wait_all(n_sub, come)
        full[sub] = jnp.sum(recv[...], axis=0)
        start_all(n_sub, share)
        local(gap + 16, gap + 32)
        wait_all(n_sub, shared)

    def reduce_crs(phase, part, recv, full, gap):
        def out(j):
            return crs_copy(phase, j, part.at[crs_peer(j)], recv.at[crs])

        def come(j):
            return crs_copy(phase, j, part.at[crs_peer(j)], recv.at[crs_from(j)])

        def share(j):
            return crs_copy(phase + 1, j, full.at[crs], full.at[crs])

        def shared(j):
            return crs_copy(phase + 1, j, full.at[crs], full.at[crs_from(j)])

        start_all(n_crs, out)
        recv[crs] = part[crs]
        local(gap, gap + 16)
        wait_all(n_crs, come)
        full[crs] = jnp.sum(recv[...], axis=0)
        start_all(n_crs, share)
        local(gap + 16, gap + 32)
        wait_all(n_crs, shared)

    reduce_crs(0, cpart, crecv, cfull, 32)
    loads[2].wait()
    coarse = stacked(cfull[...].reshape(SMP, -1))
    half_rows = coarse_v.shape[0] // 2
    for h in range(2):
        high, low = split(coarse_v[h * half_rows : (h + 1) * half_rows, :])
        inner = folded(dot_t(coarse, high)) + dot_t(coarse[:SMP], low)
        ipart[h * 8 : (h + 1) * 8] = inner.reshape(8, 8, half_rows)

    reduce_sub(2, ipart, irecv, ifull, 64)
    lifted = jnp.zeros((SMP, coarse_v.shape[1]), F32)
    for h in range(2):
        high, low = split(coarse_v[h * half_rows : (h + 1) * half_rows, :])
        inner = stacked(ifull[h * 8 : (h + 1) * 8].reshape(SMP, half_rows))
        lifted = lifted + folded(dot(inner, high)) + dot(inner[:SMP], low)
    lpart[...] = lifted.reshape(lpart.shape)

    reduce_crs(2, lpart, lrecv, lfull, 96)
    lifted = stacked(lfull[...].reshape(SMP, -1))
    for i in range(0, n_sub, 2):
        back_send[:, i * LIMIT : (i + 2) * LIMIT] = folded(
            dot(lifted, scatter_v[:, i * LIMIT : (i + 2) * LIMIT])
        )

    def back_copy(j):
        return sub_copy(4, j, lanes(back_send, sub_peer(j)), lanes(back_recv, sub))

    def back_wait(j):
        return sub_copy(4, j, lanes(back_send, sub_peer(j)), lanes(back_recv, sub_from(j)))

    start_all(n_sub, back_copy)
    back_recv[:, own] = back_send[:, own]
    wait_all(n_sub, back_wait)
    slot_v[...] = stacked(folded(dot(stacked(back_recv[...]), place_v[...])))

    dots_ref[...] = jnp.zeros_like(dots_ref)

    def lift(i):
        at = pl.multiple_of(i * chunk, chunk)
        span = pl.ds(at, chunk)
        hot = one_hot(lax.broadcasted_iota(jnp.int32, (slots, chunk), 0) == slot_ref[:, span])
        inside = pl.ds(pl.multiple_of(at + halo, BS), chunk)
        z = ext_v[:, inside] + weight_ref[:, span] * folded(dot(slot_v[...], hot))
        ext_v[:, inside] = z
        product = z * src_v[:, span]
        total = product[:, :BS]
        for k in range(1, chunk // BS):
            total = total + product[:, k * BS : (k + 1) * BS]
        dots_ref[0] += total

    chunks = nodes // chunk

    @pl.loop(0, 2)
    def _(i):
        lift(i * (chunks - 1))

    halo_now = halo_copies(ext_v, 2)
    for copy in halo_now:
        copy.start()

    @pl.loop(1, chunks - 1)
    def _(i):
        lift(i)

    store_z = pltpu.make_async_copy(ext_v.at[:, pl.ds(halo, nodes)], z_hbm, store_sem.at[0])
    store_z.start()
    for copy in cond_copies:
        copy.wait()
    for copy in halo_now:
        copy.wait()

    lane = lax.broadcasted_iota(jnp.int32, (1, BS), 1)

    def operator(b):
        at = pl.multiple_of(b * BS, BS)
        inside = pl.ds(pl.multiple_of(at + halo, BS), BS)
        v = ext_v[:, inside]
        cond = cond_v[:, inside]
        diagonal = kappa_ref[:, pl.ds(at, BS)]
        up = jnp.where(lane < BS - 1, 0.5 * (cond + pltpu.roll(cond, BS - 1, 1)), 0.0)
        down = jnp.where(lane > 0, 0.5 * (cond + pltpu.roll(cond, 1, 1)), 0.0)
        diagonal = diagonal + up + down
        taken = up * pltpu.roll(v, BS - 1, 1) + down * pltpu.roll(v, 1, 1)
        for k in range(4):
            other = pl.ds(partner_ref[b * 4 + k] * BS, BS)
            weight = 0.5 * (cond + cond_v[:, other])
            diagonal = diagonal + weight
            taken = taken + weight * ext_v[:, other]
        image = diagonal * v - taken
        q_v[:, pl.ds(at, BS)] = image
        dots_ref[1] += v * image

    @pl.loop(0, blocks // 2)
    def _(g):
        operator(g * 2)
        operator(g * 2 + 1)

    store_q = pltpu.make_async_copy(q_v, q_hbm, store_sem.at[1])
    store_q.start()
    store_z.wait()
    store_q.wait()


def apply_call(n_sub, n_crs, src, factor, coarse_factor, weight, kappa, cond, slot, owner, row, partner):
    nodes = src.shape[1]
    blocks = factor.shape[0]
    slots = owner.shape[1]
    rows, cols = coarse_factor.shape
    halo = HALO * BS
    vmem = pl.BlockSpec(memory_space=pltpu.VMEM)
    anywhere = pl.BlockSpec(memory_space=pl.ANY)
    wide = n_sub * LIMIT
    field = jax.ShapeDtypeStruct(src.shape, F32)
    return pl.pallas_call(
        functools.partial(apply_kernel, n_sub, n_crs),
        out_shape=(field, field, jax.ShapeDtypeStruct((2, SMP, BS), F32)),
        in_specs=[anywhere] * 3 + [vmem] * 6 + [pl.BlockSpec(memory_space=pltpu.SMEM)],
        out_specs=(anywhere, anywhere, vmem),
        scratch_shapes=[
            pltpu.VMEM((SMP, nodes), F32),
            pltpu.VMEM((blocks, BS, BS), F32),
            pltpu.VMEM((rows, cols), F32),
            pltpu.VMEM((SMP, nodes + 2 * halo), F32),
            pltpu.VMEM((1, nodes + 2 * halo), F32),
            pltpu.VMEM((SMP, nodes), F32),
            pltpu.VMEM((2 * SMP, slots), F32),
            pltpu.VMEM((wide, slots), BF16),
            pltpu.VMEM((cols, wide), BF16),
            pltpu.VMEM((n_sub, 8, LIMIT), F32),
            pltpu.VMEM((n_sub, 8, LIMIT), F32),
            pltpu.VMEM((SMP, wide), F32),
            pltpu.VMEM((SMP, wide), F32),
            pltpu.VMEM((SMP, wide), F32),
            pltpu.VMEM((SMP, wide), F32),
            pltpu.VMEM((n_crs, 8, cols), F32),
            pltpu.VMEM((n_crs, 8, cols), F32),
            pltpu.VMEM((n_crs, 8, cols), F32),
            pltpu.VMEM((n_sub, 8, rows // 2), F32),
            pltpu.VMEM((n_sub, 8, rows // 2), F32),
            pltpu.VMEM((n_sub, 8, rows // 2), F32),
            pltpu.VMEM((n_crs, 8, cols), F32),
            pltpu.VMEM((n_crs, 8, cols), F32),
            pltpu.VMEM((n_crs, 8, cols), F32),
            pltpu.VMEM((2 * SMP, slots), BF16),
            pltpu.SemaphoreType.DMA((3,)),
            pltpu.SemaphoreType.DMA((2,)),
            pltpu.SemaphoreType.DMA((5, n_sub)),
            pltpu.SemaphoreType.DMA((5, n_sub)),
            pltpu.SemaphoreType.DMA((4, n_crs)),
            pltpu.SemaphoreType.DMA((4, n_crs)),
            pltpu.SemaphoreType.DMA((4,)),
            pltpu.SemaphoreType.DMA((4,)),
        ],
        compiler_params=pltpu.CompilerParams(
            collective_id=0, has_side_effects=True, vmem_limit_bytes=52 * 1024 * 1024
        ),
    )(src, factor, coarse_factor, weight, kappa, cond, slot, owner, row, partner)


def scalar_kernel(n_sub, n_crs, first_ref, second_ref, out_ref, mine, crs_in, part, sub_in, crs_send, crs_recv, sub_send, sub_recv):
    sub = lax.axis_index("sub")
    crs = lax.axis_index("crs")

    def sub_peer(j):
        return lax.rem(sub + j, n_sub)

    def crs_peer(j):
        return lax.rem(crs + j, n_crs)

    barrier = pltpu.get_barrier_semaphore()

    @pl.loop(1, n_sub)
    def _(j):
        pl.semaphore_signal(barrier, inc=1, device_id=(sub_peer(j), crs), device_id_type=MESH)

    @pl.loop(1, n_crs)
    def _(j):
        pl.semaphore_signal(barrier, inc=1, device_id=(sub, crs_peer(j)), device_id_type=MESH)

    kind = lax.broadcasted_iota(jnp.int32, (8, SMP), 0)
    packed = jnp.zeros((8, SMP), F32)
    ones = jnp.ones((8, BS), F32)
    for i in range(4):
        values = (first_ref if i < 2 else second_ref)[i % 2]
        sums = lax.dot_general(
            ones,
            values,
            (((1,), (1,)), ((), ())),
            precision=lax.Precision.HIGHEST,
            preferred_element_type=F32,
        )
        packed = jnp.where(kind == i, sums, packed)
    mine[:, :SMP] = packed
    mine[:, SMP:] = jnp.zeros((8, BS - SMP), F32)
    pl.semaphore_wait(barrier, n_sub + n_crs - 2)

    def crs_copy(j, slot):
        return pltpu.make_async_remote_copy(
            src_ref=mine,
            dst_ref=crs_in.at[slot],
            send_sem=crs_send.at[j],
            recv_sem=crs_recv.at[j],
            device_id=(sub, crs_peer(j)),
            device_id_type=MESH,
        )

    def sub_copy(j, slot):
        return pltpu.make_async_remote_copy(
            src_ref=part,
            dst_ref=sub_in.at[slot],
            send_sem=sub_send.at[j],
            recv_sem=sub_recv.at[j],
            device_id=(sub_peer(j), crs),
            device_id_type=MESH,
        )

    @pl.loop(1, n_crs)
    def _(j):
        crs_copy(j, crs).start()

    crs_in[crs] = mine[...]

    @pl.loop(1, n_crs)
    def _(j):
        crs_copy(j, lax.rem(crs + n_crs - j, n_crs)).wait()

    part[...] = jnp.sum(crs_in[...], axis=0)

    @pl.loop(1, n_sub)
    def _(j):
        sub_copy(j, sub).start()

    sub_in[sub] = part[...]

    @pl.loop(1, n_sub)
    def _(j):
        sub_copy(j, lax.rem(sub + n_sub - j, n_sub)).wait()

    out_ref[...] = jnp.sum(sub_in[...], axis=0)


def scalar_call(n_sub, n_crs, first, second):
    vmem = pl.BlockSpec(memory_space=pltpu.VMEM)
    return pl.pallas_call(
        functools.partial(scalar_kernel, n_sub, n_crs),
        out_shape=jax.ShapeDtypeStruct((8, BS), F32),
        in_specs=[vmem] * 2,
        out_specs=vmem,
        scratch_shapes=[
            pltpu.VMEM((8, BS), F32),
            pltpu.VMEM((n_crs, 8, BS), F32),
            pltpu.VMEM((8, BS), F32),
            pltpu.VMEM((n_sub, 8, BS), F32),
            pltpu.SemaphoreType.DMA((n_crs,)),
            pltpu.SemaphoreType.DMA((n_crs,)),
            pltpu.SemaphoreType.DMA((n_sub,)),
            pltpu.SemaphoreType.DMA((n_sub,)),
        ],
        compiler_params=pltpu.CompilerParams(collective_id=1, has_side_effects=True),
    )(first, second)


def solution(mesh):
    n_sub, n_crs = mesh.shape["sub"], mesh.shape["crs"]

    def per_device(
        right_side,
        kappa_sq,
        conduct,
        partners,
        local_factor,
        restrict_weight,
        aggregate,
        owner,
        owner_coarse_row,
        coarse_factor,
    ):
        nodes = right_side.shape[1]
        slots = owner.shape[0]
        first_block = lax.axis_index(("sub", "crs")) * local_factor.shape[0] - HALO
        rest = (
            local_factor,
            coarse_factor,
            restrict_weight.reshape(1, nodes),
            kappa_sq.reshape(1, nodes),
            conduct.reshape(1, nodes),
            aggregate,
            owner.reshape(1, slots),
            owner_coarse_row.reshape(1, slots),
            (partners - first_block).reshape(-1),
        )
        z, q, first = apply_call(n_sub, n_crs, right_side, *rest)
        u, t, second = apply_call(n_sub, n_crs, q, *rest)
        sums = scalar_call(n_sub, n_crs, first, second)
        rz, zq, qu, ut = (sums[i, :SMP] for i in range(4))
        step = rz / zq
        rz_next = step * step * qu - rz
        ratio = rz_next / rz
        grown = 1.0 + ratio
        curvature = grown * grown * zq - 2.0 * grown * step * qu + step * step * ut
        step_next = rz_next / curvature
        near = (step + step_next * grown)[:, None]
        far = (step * step_next)[:, None]
        return near * z - far * u, right_side - near * q + far * t

    return jax.shard_map(
        per_device,
        mesh=mesh,
        in_specs=(
            P(None, ("sub", "crs")),
            P(("sub", "crs")),
            P(("sub", "crs")),
            P(("sub", "crs"), None),
            P(("sub", "crs"), None, None),
            P(("sub", "crs")),
            P(("sub", "crs"), None),
            P(("sub", "crs"), None),
            P(("sub", "crs")),
            P("crs", "sub"),
        ),
        out_specs=(P(None, ("sub", "crs")), P(None, ("sub", "crs"))),
        check_vma=False,
    )
```

```python
import functools

import jax
import jax.numpy as jnp
from jax import lax
from jax.experimental import pallas as pl
from jax.experimental.pallas import tpu as pltpu
from jax.sharding import PartitionSpec as P

MESH = pl.DeviceIdType.MESH
F32 = jnp.float32
BF16 = jnp.bfloat16
HALO = 7
BS = 128
SMP = 64
LIMIT = 128
VMEM_LIMIT = 40


def split(x):
    high = x.astype(BF16)
    return high, (x - high.astype(F32)).astype(BF16)


def dot(a, b):
    return lax.dot_general(a, b, (((1,), (0,)), ((), ())), preferred_element_type=F32)


def dot_t(a, b):
    return lax.dot_general(a, b, (((1,), (1,)), ((), ())), preferred_element_type=F32)


def stacked(x):
    return jnp.concatenate(split(x), axis=0)


def folded(y):
    half = y.shape[0] // 2
    return y[:half] + y[half:]


def one_hot(mask):
    return jnp.where(mask, 1.0, 0.0).astype(BF16)


def apply_kernel(
    n_sub,
    n_crs,
    src_hbm,
    factor_hbm,
    coarse_hbm,
    weight_hbm,
    kappa_hbm,
    cond_hbm,
    slot_hbm,
    owner_hbm,
    row_hbm,
    partner_ref,
    image_one,
    image_two,
    ext_one,
    ext_two,
    weight_ref,
    kappa_ref,
    slot_ref,
    owner_ref,
    row_ref,
    coarse_high,
    coarse_low,
    src_v,
    factor_v,
    coarse_v,
    cond_v,
    acc_v,
    place_v,
    scatter_v,
    index_send,
    index_recv,
    slot_send,
    slot_recv,
    back_send,
    back_recv,
    cpart,
    crecv,
    cfull,
    ipart,
    irecv,
    ifull,
    lpart,
    lrecv,
    lfull,
    slot_v,
    rates_v,
    dots_ref,
    sums_mine,
    sums_crs,
    sums_part,
    sums_sub,
    load_sem,
    sub_send,
    sub_recv,
    crs_send,
    crs_recv,
    halo_send,
    halo_recv,
):
    sub = lax.axis_index("sub")
    crs = lax.axis_index("crs")
    me = sub * n_crs + crs
    total = n_sub * n_crs
    right = lax.rem(me + 1, total)
    left = lax.rem(me + total - 1, total)
    nodes = src_v.shape[1]
    blocks = nodes // BS
    slots = owner_ref.shape[1]
    halo = HALO * BS

    def sub_peer(j):
        return lax.rem(sub + j, n_sub)

    def sub_from(j):
        return lax.rem(sub + n_sub - j, n_sub)

    def crs_peer(j):
        return lax.rem(crs + j, n_crs)

    def crs_from(j):
        return lax.rem(crs + n_crs - j, n_crs)

    def at_device(d):
        return (d // n_crs, lax.rem(d, n_crs))

    def sub_copy(phase, j, source, target):
        return pltpu.make_async_remote_copy(
            src_ref=source,
            dst_ref=target,
            send_sem=sub_send.at[phase, j],
            recv_sem=sub_recv.at[phase, j],
            device_id=(sub_peer(j), crs),
            device_id_type=MESH,
        )

    def crs_copy(phase, j, source, target):
        return pltpu.make_async_remote_copy(
            src_ref=source,
            dst_ref=target,
            send_sem=crs_send.at[phase, j],
            recv_sem=crs_recv.at[phase, j],
            device_id=(sub, crs_peer(j)),
            device_id_type=MESH,
        )

    def lanes(ref, i):
        return ref.at[:, pl.ds(pl.multiple_of(i * LIMIT, LIMIT), LIMIT)]

    def start_all(count, copy):
        @pl.loop(1, count)
        def _(j):
            copy(j).start()

    def wait_all(count, copy):
        @pl.loop(1, count)
        def _(j):
            copy(j).wait()

    loads = [
        pltpu.make_async_copy(src_hbm, src_v, load_sem.at[0]),
        pltpu.make_async_copy(factor_hbm, factor_v, load_sem.at[1]),
        pltpu.make_async_copy(coarse_hbm, coarse_v, load_sem.at[2]),
        pltpu.make_async_copy(weight_hbm, weight_ref, load_sem.at[3]),
        pltpu.make_async_copy(slot_hbm, slot_ref, load_sem.at[4]),
        pltpu.make_async_copy(owner_hbm, owner_ref, load_sem.at[5]),
        pltpu.make_async_copy(row_hbm, row_ref, load_sem.at[6]),
        pltpu.make_async_copy(cond_hbm, cond_v.at[:, pl.ds(halo, nodes)], load_sem.at[7]),
        pltpu.make_async_copy(kappa_hbm, kappa_ref, load_sem.at[8]),
    ]
    for i in (5, 6, 7, 3, 4, 0, 8, 1, 2):
        loads[i].start()

    barrier = pltpu.get_barrier_semaphore()

    @pl.loop(1, n_sub)
    def _(j):
        pl.semaphore_signal(barrier, inc=1, device_id=(sub_peer(j), crs), device_id_type=MESH)

    @pl.loop(1, n_crs)
    def _(j):
        pl.semaphore_signal(barrier, inc=1, device_id=(sub, crs_peer(j)), device_id_type=MESH)

    pl.semaphore_signal(barrier, inc=1, device_id=at_device(left), device_id_type=MESH)
    pl.semaphore_signal(barrier, inc=1, device_id=at_device(right), device_id_type=MESH)

    loads[5].wait()
    loads[6].wait()
    owner_row = owner_ref[...]
    group = lax.broadcasted_iota(jnp.int32, (n_sub, slots), 0)
    members = jnp.where(owner_row == group, 1.0, 0.0)
    before = one_hot(
        lax.broadcasted_iota(jnp.int32, (slots, slots), 0)
        < lax.broadcasted_iota(jnp.int32, (slots, slots), 1)
    )
    ahead = dot(members.astype(BF16), before)
    rank = jnp.sum(members * ahead, axis=0, keepdims=True)
    place = owner_row * LIMIT + rank.astype(jnp.int32)
    row_one = stacked(jnp.broadcast_to((row_ref[...] + 1).astype(F32), (8, slots)))

    @pl.loop(0, n_sub)
    def _(i):
        start = pl.multiple_of(i * LIMIT, LIMIT)
        hot = one_hot(lax.broadcasted_iota(jnp.int32, (LIMIT, slots), 0) + start == place)
        place_v[pl.ds(start, LIMIT), :] = hot
        index_send[i] = folded(dot_t(row_one, hot)) - 1.0

    loads[7].wait()
    index_recv[sub] = index_send[sub]

    pl.semaphore_wait(barrier, n_sub + n_crs)

    def index_copy(j):
        return sub_copy(0, j, index_send.at[sub_peer(j)], index_recv.at[sub])

    def index_wait(j):
        return sub_copy(0, j, index_send.at[sub_peer(j)], index_recv.at[sub_from(j)])

    start_all(n_sub, index_copy)

    def halo_copies(buffer, phase):
        up = pltpu.make_async_remote_copy(
            src_ref=buffer.at[:, pl.ds(nodes, halo)],
            dst_ref=buffer.at[:, pl.ds(0, halo)],
            send_sem=halo_send.at[phase],
            recv_sem=halo_recv.at[phase],
            device_id=at_device(right),
            device_id_type=MESH,
        )
        down = pltpu.make_async_remote_copy(
            src_ref=buffer.at[:, pl.ds(halo, halo)],
            dst_ref=buffer.at[:, pl.ds(halo + nodes, halo)],
            send_sem=halo_send.at[phase + 1],
            recv_sem=halo_recv.at[phase + 1],
            device_id=at_device(left),
            device_id_type=MESH,
        )
        return up, down

    cond_copies = halo_copies(cond_v, 0)
    for copy in cond_copies:
        copy.start()

    half_rows = coarse_v.shape[0] // 2
    own = pl.ds(pl.multiple_of(sub * LIMIT, LIMIT), LIMIT)
    chunk = 1024
    chunks = nodes // chunk
    lane = lax.broadcasted_iota(jnp.int32, (1, BS), 1)
    dots_ref[...] = jnp.zeros_like(dots_ref)

    def apply(turn, src_v, ext_v, q_v):
        if turn == 0:
            loads[3].wait()
            loads[4].wait()
            loads[0].wait()
        acc_v[...] = jnp.zeros_like(acc_v)

        wide = 2048

        @pl.loop(0, nodes // wide)
        def _(i):
            span = pl.ds(pl.multiple_of(i * wide, wide), wide)
            weighted = src_v[:, span] * weight_ref[:, span]
            hot = one_hot(lax.broadcasted_iota(jnp.int32, (slots, wide), 0) == slot_ref[:, span])
            acc_v[...] += dot_t(hot, stacked(weighted))

        tiles = stacked(folded(jnp.transpose(acc_v[...])))
        for i in range(0, n_sub, 2):
            slot_send[:, i * LIMIT : (i + 2) * LIMIT] = folded(
                dot_t(tiles, place_v[i * LIMIT : (i + 2) * LIMIT, :])
            )

        def slot_copy(j):
            return sub_copy(5 * turn + 1, j, lanes(slot_send, sub_peer(j)), lanes(slot_recv, sub))

        def slot_wait(j):
            return sub_copy(5 * turn + 1, j, lanes(slot_send, sub_peer(j)), lanes(slot_recv, sub_from(j)))

        start_all(n_sub, slot_copy)
        slot_recv[:, own] = slot_send[:, own]

        def local(first, last):
            @pl.loop(first // 4, last // 4)
            def _(g):
                for k in range(4):
                    b = g * 4 + k
                    at = pl.multiple_of(b * BS, BS)
                    values = stacked(src_v[:, pl.ds(at, BS)])
                    high, low = split(factor_v[b])
                    half = folded(dot(values, high)) + dot(values[:SMP], low)
                    half = stacked(half)
                    ext_v[:, pl.ds(pl.multiple_of(at + halo, BS), BS)] = folded(
                        dot_t(half, high)
                    ) + dot_t(half[:SMP], low)

        if turn == 0:
            loads[1].wait()
        local(0, 32)

        if turn == 0:
            wait_all(n_sub, index_wait)

            @pl.loop(0, n_sub)
            def _(i):
                index = index_recv[i][0:1, :].astype(jnp.int32)
                rows = scatter_v.shape[0]
                span = pl.ds(pl.multiple_of(i * LIMIT, LIMIT), LIMIT)
                scatter_v[:, span] = one_hot(lax.broadcasted_iota(jnp.int32, (rows, LIMIT), 0) == index)

        if turn == 0:
            loads[2].wait()
            step_rows = 128

            @pl.loop(0, coarse_v.shape[0] // step_rows)
            def _(i):
                span = pl.ds(pl.multiple_of(i * step_rows, step_rows), step_rows)
                high, low = split(coarse_v[span, :])
                coarse_high[span, :] = high
                coarse_low[span, :] = low

        wait_all(n_sub, slot_wait)
        coarse_part = folded(dot_t(stacked(slot_recv[...]), scatter_v[...]))
        cpart[...] = coarse_part.reshape(cpart.shape)

        def reduce_sub(phase, part, recv, full, gap):
            def out(j):
                return sub_copy(phase, j, part.at[sub_peer(j)], recv.at[sub])

            def come(j):
                return sub_copy(phase, j, part.at[sub_peer(j)], recv.at[sub_from(j)])

            def share(j):
                return sub_copy(phase + 1, j, full.at[sub], full.at[sub])

            def shared(j):
                return sub_copy(phase + 1, j, full.at[sub], full.at[sub_from(j)])

            start_all(n_sub, out)
            recv[sub] = part[sub]
            local(gap, gap + 16)
            wait_all(n_sub, come)
            full[sub] = jnp.sum(recv[...], axis=0)
            start_all(n_sub, share)
            local(gap + 16, gap + 32)
            wait_all(n_sub, shared)

        def reduce_crs(phase, part, recv, full, gap):
            def out(j):
                return crs_copy(phase, j, part.at[crs_peer(j)], recv.at[crs])

            def come(j):
                return crs_copy(phase, j, part.at[crs_peer(j)], recv.at[crs_from(j)])

            def share(j):
                return crs_copy(phase + 1, j, full.at[crs], full.at[crs])

            def shared(j):
                return crs_copy(phase + 1, j, full.at[crs], full.at[crs_from(j)])

            start_all(n_crs, out)
            recv[crs] = part[crs]
            local(gap, gap + 16)
            wait_all(n_crs, come)
            full[crs] = jnp.sum(recv[...], axis=0)
            start_all(n_crs, share)
            local(gap + 16, gap + 32)
            wait_all(n_crs, shared)

        reduce_crs(4 * turn, cpart, crecv, cfull, 32)
        coarse = stacked(cfull[...].reshape(SMP, -1))
        for h in range(2):
            high = coarse_high[h * half_rows : (h + 1) * half_rows, :]
            low = coarse_low[h * half_rows : (h + 1) * half_rows, :]
            inner = folded(dot_t(coarse, high)) + dot_t(coarse[:SMP], low)
            ipart[h * 8 : (h + 1) * 8] = inner.reshape(8, 8, half_rows)

        reduce_sub(5 * turn + 2, ipart, irecv, ifull, 64)
        lifted = jnp.zeros((SMP, coarse_v.shape[1]), F32)
        for h in range(2):
            high = coarse_high[h * half_rows : (h + 1) * half_rows, :]
            low = coarse_low[h * half_rows : (h + 1) * half_rows, :]
            inner = stacked(ifull[h * 8 : (h + 1) * 8].reshape(SMP, half_rows))
            lifted = lifted + folded(dot(inner, high)) + dot(inner[:SMP], low)
        lpart[...] = lifted.reshape(lpart.shape)

        reduce_crs(4 * turn + 2, lpart, lrecv, lfull, 96)
        lifted = stacked(lfull[...].reshape(SMP, -1))
        for i in range(0, n_sub, 2):
            back_send[:, i * LIMIT : (i + 2) * LIMIT] = folded(
                dot(lifted, scatter_v[:, i * LIMIT : (i + 2) * LIMIT])
            )

        def back_copy(j):
            return sub_copy(5 * turn + 4, j, lanes(back_send, sub_peer(j)), lanes(back_recv, sub))

        def back_wait(j):
            return sub_copy(5 * turn + 4, j, lanes(back_send, sub_peer(j)), lanes(back_recv, sub_from(j)))

        start_all(n_sub, back_copy)
        back_recv[:, own] = back_send[:, own]
        if turn == 0:
            for copy in cond_copies:
                copy.wait()
            loads[8].wait()

            @pl.loop(0, blocks)
            def _(b):
                at = pl.multiple_of(b * BS, BS)
                cond = cond_v[:, pl.ds(pl.multiple_of(at + halo, BS), BS)]
                up = jnp.where(lane < BS - 1, 0.5 * (cond + pltpu.roll(cond, BS - 1, 1)), 0.0)
                down = jnp.where(lane > 0, 0.5 * (cond + pltpu.roll(cond, 1, 1)), 0.0)
                whole = kappa_ref[:, pl.ds(at, BS)] + up + down
                for k in range(4):
                    other = pl.ds(partner_ref[k * blocks + b] * BS, BS)
                    weight = 0.5 * (cond + cond_v[:, other])
                    rates_v[b, k : k + 1] = weight
                    whole = whole + weight
                rates_v[b, 4:5] = whole
                rates_v[b, 5:6] = up
                rates_v[b, 6:7] = down

        wait_all(n_sub, back_wait)
        slot_v[...] = stacked(folded(dot(stacked(back_recv[...]), place_v[...])))

        def lift(i):
            at = pl.multiple_of(i * chunk, chunk)
            span = pl.ds(at, chunk)
            hot = one_hot(lax.broadcasted_iota(jnp.int32, (slots, chunk), 0) == slot_ref[:, span])
            inside = pl.ds(pl.multiple_of(at + halo, BS), chunk)
            z = ext_v[:, inside] + weight_ref[:, span] * folded(dot(slot_v[...], hot))
            ext_v[:, inside] = z
            product = z * src_v[:, span]
            total = product[:, :BS]
            for k in range(1, chunk // BS):
                total = total + product[:, k * BS : (k + 1) * BS]
            dots_ref[2 * turn] += total

        @pl.loop(0, 2)
        def _(i):
            lift(i * (chunks - 1))

        halo_now = halo_copies(ext_v, 2 + 2 * turn)
        for copy in halo_now:
            copy.start()

        @pl.loop(1, chunks - 1)
        def _(i):
            lift(i)

        for copy in halo_now:
            copy.wait()

        per_turn = 4

        def operator(g, total):
            images = []
            for i in range(per_turn):
                b = g * per_turn + i
                v = ext_v[:, pl.ds(pl.multiple_of(b * BS + halo, BS), BS)]
                rates = rates_v[b]
                image = rates[4:5] * v
                image = image - rates[5:6] * pltpu.roll(v, BS - 1, 1)
                image = image - rates[6:7] * pltpu.roll(v, 1, 1)
                for k in range(4):
                    other = pl.ds(partner_ref[k * blocks + b] * BS, BS)
                    image = image - rates[k : k + 1] * ext_v[:, other]
                images.append(image)
                total = total + v * image
            for i in range(per_turn):
                at = pl.multiple_of((g * per_turn + i) * BS, BS)
                q_v[:, pl.ds(at, BS)] = images[i]
            return total

        dots_ref[2 * turn + 1] = lax.fori_loop(
            0, blocks // per_turn, operator, jnp.zeros((SMP, BS), F32)
        )

    apply(0, src_v, ext_one, image_one)
    apply(1, image_one, ext_two, image_two)

    kind = lax.broadcasted_iota(jnp.int32, (8, BS), 0)
    packed = jnp.zeros((8, BS), F32)
    ones = jnp.ones((8, BS), F32)
    for i in range(4):
        sums = lax.dot_general(
            ones,
            jnp.concatenate([dots_ref[i], jnp.zeros((BS - SMP, BS), F32)], axis=0),
            (((1,), (1,)), ((), ())),
            precision=lax.Precision.HIGHEST,
            preferred_element_type=F32,
        )
        packed = jnp.where(kind == i, sums, packed)
    sums_mine[...] = packed

    def sums_out(j):
        return crs_copy(8, j, sums_mine, sums_crs.at[crs])

    def sums_come(j):
        return crs_copy(8, j, sums_mine, sums_crs.at[crs_from(j)])

    def part_out(j):
        return sub_copy(10, j, sums_part, sums_sub.at[sub])

    def part_come(j):
        return sub_copy(10, j, sums_part, sums_sub.at[sub_from(j)])

    start_all(n_crs, sums_out)
    sums_crs[crs] = sums_mine[...]
    wait_all(n_crs, sums_come)
    sums_part[...] = jnp.sum(sums_crs[...], axis=0)
    start_all(n_sub, part_out)
    sums_sub[sub] = sums_part[...]
    wait_all(n_sub, part_come)
    sums = jnp.sum(sums_sub[...], axis=0)
    rz, zq, qu, ut = (sums[i : i + 1] for i in range(4))
    step = rz / zq
    rz_next = step * step * qu - rz
    ratio = rz_next / rz
    grown = 1.0 + ratio
    curvature = grown * grown * zq - 2.0 * grown * step * qu + step * step * ut
    step_next = rz_next / curvature
    near = jnp.transpose(jnp.broadcast_to(step + step_next * grown, (BS, BS)))[:SMP]
    far = jnp.transpose(jnp.broadcast_to(step * step_next, (BS, BS)))[:SMP]

    @pl.loop(0, blocks // 2)
    def _(g):
        for k in range(2):
            at = pl.multiple_of((g * 2 + k) * BS, BS)
            span = pl.ds(at, BS)
            inside = pl.ds(pl.multiple_of(at + halo, BS), BS)
            residual = src_v[:, span] - near * image_one[:, span] + far * image_two[:, span]
            image_one[:, span] = near * ext_one[:, inside] - far * ext_two[:, inside]
            image_two[:, span] = residual


def apply_call(n_sub, n_crs, src, factor, coarse_factor, weight, kappa, cond, slot, owner, row, partner):
    nodes = src.shape[1]
    blocks = factor.shape[0]
    slots = owner.shape[1]
    rows, cols = coarse_factor.shape
    halo = HALO * BS
    vmem = pl.BlockSpec(memory_space=pltpu.VMEM)
    anywhere = pl.BlockSpec(memory_space=pltpu.HBM)
    wide = n_sub * LIMIT
    field = jax.ShapeDtypeStruct(src.shape, F32)
    return pl.pallas_call(
        functools.partial(apply_kernel, n_sub, n_crs),
        out_shape=(field, field),
        in_specs=[anywhere] * 9 + [pl.BlockSpec(memory_space=pltpu.SMEM)],
        out_specs=(vmem,) * 2,
        scratch_shapes=[
            pltpu.VMEM((SMP, nodes + 2 * halo), F32),
            pltpu.VMEM((SMP, nodes + 2 * halo), F32),
            pltpu.VMEM((1, nodes), F32),
            pltpu.VMEM((1, nodes), F32),
            pltpu.VMEM((1, nodes), jnp.int32),
            pltpu.VMEM((1, slots), jnp.int32),
            pltpu.VMEM((1, slots), jnp.int32),
            pltpu.VMEM((rows, cols), BF16),
            pltpu.VMEM((rows, cols), BF16),
            pltpu.VMEM((SMP, nodes), F32),
            pltpu.VMEM((blocks, BS, BS), F32),
            pltpu.VMEM((rows, cols), F32),
            pltpu.VMEM((1, nodes + 2 * halo), F32),
            pltpu.VMEM((slots, 2 * SMP), F32),
            pltpu.VMEM((wide, slots), BF16),
            pltpu.VMEM((cols, wide), BF16),
            pltpu.VMEM((n_sub, 8, LIMIT), F32),
            pltpu.VMEM((n_sub, 8, LIMIT), F32),
            pltpu.VMEM((SMP, wide), F32),
            pltpu.VMEM((SMP, wide), F32),
            pltpu.VMEM((SMP, wide), F32),
            pltpu.VMEM((SMP, wide), F32),
            pltpu.VMEM((n_crs, 8, cols), F32),
            pltpu.VMEM((n_crs, 8, cols), F32),
            pltpu.VMEM((n_crs, 8, cols), F32),
            pltpu.VMEM((n_sub, 8, rows // 2), F32),
            pltpu.VMEM((n_sub, 8, rows // 2), F32),
            pltpu.VMEM((n_sub, 8, rows // 2), F32),
            pltpu.VMEM((n_crs, 8, cols), F32),
            pltpu.VMEM((n_crs, 8, cols), F32),
            pltpu.VMEM((n_crs, 8, cols), F32),
            pltpu.VMEM((2 * SMP, slots), BF16),
            pltpu.VMEM((blocks, 8, BS), F32),
            pltpu.VMEM((4, SMP, BS), F32),
            pltpu.VMEM((8, BS), F32),
            pltpu.VMEM((n_crs, 8, BS), F32),
            pltpu.VMEM((8, BS), F32),
            pltpu.VMEM((n_sub, 8, BS), F32),
            pltpu.SemaphoreType.DMA((9,)),
            pltpu.SemaphoreType.DMA((11, n_sub)),
            pltpu.SemaphoreType.DMA((11, n_sub)),
            pltpu.SemaphoreType.DMA((9, n_crs)),
            pltpu.SemaphoreType.DMA((9, n_crs)),
            pltpu.SemaphoreType.DMA((6,)),
            pltpu.SemaphoreType.DMA((6,)),
        ],
        compiler_params=pltpu.CompilerParams(
            collective_id=0, has_side_effects=True, vmem_limit_bytes=VMEM_LIMIT * 1024 * 1024
        ),
    )(src, factor, coarse_factor, weight, kappa, cond, slot, owner, row, partner)


def solution(mesh):
    n_sub, n_crs = mesh.shape["sub"], mesh.shape["crs"]

    def per_device(
        right_side,
        kappa_sq,
        conduct,
        partners,
        local_factor,
        restrict_weight,
        aggregate,
        owner,
        owner_coarse_row,
        coarse_factor,
    ):
        nodes = right_side.shape[1]
        slots = owner.shape[0]
        first_block = lax.axis_index(("sub", "crs")) * local_factor.shape[0] - HALO
        rest = (
            local_factor,
            coarse_factor,
            restrict_weight.reshape(1, nodes),
            kappa_sq.reshape(1, nodes),
            conduct.reshape(1, nodes),
            aggregate,
            owner.reshape(1, slots),
            owner_coarse_row.reshape(1, slots),
            (partners.T - first_block).reshape(-1),
        )
        return apply_call(n_sub, n_crs, right_side, *rest)

    return jax.shard_map(
        per_device,
        mesh=mesh,
        in_specs=(
            P(None, ("sub", "crs")),
            P(("sub", "crs")),
            P(("sub", "crs")),
            P(("sub", "crs"), None),
            P(("sub", "crs"), None, None),
            P(("sub", "crs")),
            P(("sub", "crs"), None),
            P(("sub", "crs"), None),
            P(("sub", "crs")),
            P("crs", "sub"),
        ),
        out_specs=(P(None, ("sub", "crs")), P(None, ("sub", "crs"))),
        check_vma=False,
    )
```

```python
import functools

import jax
import jax.numpy as jnp
from jax import lax
from jax.experimental import pallas as pl
from jax.experimental.pallas import tpu as pltpu
from jax.sharding import PartitionSpec as P

MESH = pl.DeviceIdType.MESH
F32 = jnp.float32
BF16 = jnp.bfloat16
HALO = 7
BS = 128
SMP = 64
LIMIT = 128
RING = 4
CORES = 2
VMEM_LIMIT = 40


def split(x):
    high = x.astype(BF16)
    return high, (x - high.astype(F32)).astype(BF16)


def dot(a, b):
    return lax.dot_general(a, b, (((1,), (0,)), ((), ())), preferred_element_type=F32)


def dot_t(a, b):
    return lax.dot_general(a, b, (((1,), (1,)), ((), ())), preferred_element_type=F32)


def stacked(x):
    return jnp.concatenate(split(x), axis=0)


def folded(y):
    half = y.shape[0] // 2
    return y[:half] + y[half:]


def farthest_first(count, depth):
    width = count // depth

    def hops(j):
        outer, inner = j // depth, j % depth
        return 2 * min(outer, width - outer) + 2 * min(inner, depth - inner) * (depth > CORES)

    return sorted(range(1, count), key=lambda j: (-hops(j), j))


def one_hot(mask):
    return jnp.where(mask, 1.0, 0.0).astype(BF16)


def apply_kernel(
    n_sub,
    n_crs,
    src_hbm,
    factor_hbm,
    coarse_hbm,
    real_hbm,
    slot_hbm,
    name_hbm,
    partner_ref,
    image_one,
    image_two,
    ext_one,
    ext_two,
    weight_ref,
    kappa_ref,
    slot_ref,
    owner_ref,
    row_ref,
    coarse_high,
    coarse_low,
    src_v,
    factor_v,
    coarse_v,
    cond_v,
    acc_v,
    place_v,
    scatter_v,
    index_send,
    index_recv,
    slot_send,
    slot_recv,
    back_send,
    back_recv,
    cpart,
    crecv,
    cfull,
    ipart,
    irecv,
    ifull,
    lpart,
    lrecv,
    lfull,
    slot_v,
    rates_v,
    dots_ref,
    sums_mine,
    sums_crs,
    sums_part,
    sums_sub,
    load_sem,
    sub_send,
    sub_recv,
    crs_send,
    crs_recv,
    halo_send,
    halo_recv,
):
    sub = lax.axis_index("sub")
    crs = lax.axis_index("crs")
    me = sub * n_crs + crs
    total = n_sub * n_crs
    right = lax.rem(me + 1, total)
    left = lax.rem(me + total - 1, total)
    nodes = src_v.shape[1]
    blocks = nodes // BS
    slots = owner_ref.shape[1]
    halo = HALO * BS

    def shifted(place, j, width, depth, sign):
        outer = lax.rem(lax.div(place, depth) + width + sign * (j // depth), width)
        inner = lax.rem(lax.rem(place, depth) + depth + sign * (j % depth), depth)
        return outer * depth + inner

    def sub_peer(j):
        return shifted(sub, j, n_sub // RING, RING, 1)

    def sub_from(j):
        return shifted(sub, j, n_sub // RING, RING, -1)

    def crs_peer(j):
        return shifted(crs, j, n_crs // CORES, CORES, 1)

    def crs_from(j):
        return shifted(crs, j, n_crs // CORES, CORES, -1)

    def at_device(d):
        return (d // n_crs, lax.rem(d, n_crs))

    def sub_copy(phase, j, source, target):
        return pltpu.make_async_remote_copy(
            src_ref=source,
            dst_ref=target,
            send_sem=sub_send.at[phase, j],
            recv_sem=sub_recv.at[phase, j],
            device_id=(sub_peer(j), crs),
            device_id_type=MESH,
        )

    def crs_copy(phase, j, source, target):
        return pltpu.make_async_remote_copy(
            src_ref=source,
            dst_ref=target,
            send_sem=crs_send.at[phase, j],
            recv_sem=crs_recv.at[phase, j],
            device_id=(sub, crs_peer(j)),
            device_id_type=MESH,
        )

    def lanes(ref, i):
        return ref.at[:, pl.ds(pl.multiple_of(i * LIMIT, LIMIT), LIMIT)]

    def start_all(count, copy):
        for j in farthest_first(count, RING if count == n_sub else CORES):
            copy(j).start()

    def wait_all(count, copy):
        @pl.loop(1, count)
        def _(j):
            copy(j).wait()

    loads = [
        pltpu.make_async_copy(src_hbm, src_v, load_sem.at[0]),
        pltpu.make_async_copy(factor_hbm, factor_v, load_sem.at[1]),
        pltpu.make_async_copy(coarse_hbm, coarse_v, load_sem.at[2]),
        pltpu.make_async_copy(real_hbm.at[:, pl.ds(0, nodes)], weight_ref, load_sem.at[3]),
        pltpu.make_async_copy(slot_hbm, slot_ref, load_sem.at[4]),
        pltpu.make_async_copy(name_hbm.at[:, pl.ds(0, slots)], owner_ref, load_sem.at[5]),
        pltpu.make_async_copy(name_hbm.at[:, pl.ds(slots, slots)], row_ref, load_sem.at[6]),
        pltpu.make_async_copy(
            real_hbm.at[:, pl.ds(2 * nodes, nodes)],
            cond_v.at[:, pl.ds(halo, nodes)],
            load_sem.at[7],
        ),
        pltpu.make_async_copy(real_hbm.at[:, pl.ds(nodes, nodes)], kappa_ref, load_sem.at[8]),
    ]
    for i in (5, 6, 7, 3, 4, 0, 8, 1, 2):
        loads[i].start()

    barrier = pltpu.get_barrier_semaphore()

    @pl.loop(1, n_sub)
    def _(j):
        pl.semaphore_signal(barrier, inc=1, device_id=(sub_peer(j), crs), device_id_type=MESH)

    @pl.loop(1, n_crs)
    def _(j):
        pl.semaphore_signal(barrier, inc=1, device_id=(sub, crs_peer(j)), device_id_type=MESH)

    pl.semaphore_signal(barrier, inc=1, device_id=at_device(left), device_id_type=MESH)
    pl.semaphore_signal(barrier, inc=1, device_id=at_device(right), device_id_type=MESH)

    loads[5].wait()
    loads[6].wait()
    owner_row = owner_ref[...]
    group = lax.broadcasted_iota(jnp.int32, (n_sub, slots), 0)
    members = jnp.where(owner_row == group, 1.0, 0.0)
    before = one_hot(
        lax.broadcasted_iota(jnp.int32, (slots, slots), 0)
        < lax.broadcasted_iota(jnp.int32, (slots, slots), 1)
    )
    ahead = dot(members.astype(BF16), before)
    rank = jnp.sum(members * ahead, axis=0, keepdims=True)
    place = owner_row * LIMIT + rank.astype(jnp.int32)
    row_one = stacked(jnp.broadcast_to((row_ref[...] + 1).astype(F32), (8, slots)))

    for i in range(0, n_sub, 4):
        start = i * LIMIT
        hot = one_hot(lax.broadcasted_iota(jnp.int32, (4 * LIMIT, slots), 0) + start == place)
        place_v[start : start + 4 * LIMIT, :] = hot
        index = folded(dot_t(row_one, hot)) - 1.0
        for k in range(4):
            index_send[i + k] = index[:, k * LIMIT : (k + 1) * LIMIT]

    loads[7].wait()
    index_recv[sub] = index_send[sub]

    pl.semaphore_wait(barrier, n_sub + n_crs)

    def index_copy(j):
        return sub_copy(0, j, index_send.at[sub_peer(j)], index_recv.at[sub])

    def index_wait(j):
        return sub_copy(0, j, index_send.at[sub_peer(j)], index_recv.at[sub_from(j)])

    start_all(n_sub, index_copy)

    def halo_copies(buffer, phase):
        up = pltpu.make_async_remote_copy(
            src_ref=buffer.at[:, pl.ds(nodes, halo)],
            dst_ref=buffer.at[:, pl.ds(0, halo)],
            send_sem=halo_send.at[phase],
            recv_sem=halo_recv.at[phase],
            device_id=at_device(right),
            device_id_type=MESH,
        )
        down = pltpu.make_async_remote_copy(
            src_ref=buffer.at[:, pl.ds(halo, halo)],
            dst_ref=buffer.at[:, pl.ds(halo + nodes, halo)],
            send_sem=halo_send.at[phase + 1],
            recv_sem=halo_recv.at[phase + 1],
            device_id=at_device(left),
            device_id_type=MESH,
        )
        return up, down

    cond_copies = halo_copies(cond_v, 0)
    for copy in cond_copies:
        copy.start()

    half_rows = coarse_v.shape[0] // 2
    own = pl.ds(pl.multiple_of(sub * LIMIT, LIMIT), LIMIT)
    chunk = 1024
    chunks = nodes // chunk
    lane = lax.broadcasted_iota(jnp.int32, (1, BS), 1)
    dots_ref[...] = jnp.zeros_like(dots_ref)

    def apply(turn, src_v, ext_v, q_v):
        if turn == 0:
            loads[3].wait()
            loads[4].wait()
            loads[0].wait()
        acc_v[...] = jnp.zeros_like(acc_v)

        wide = 2048

        @pl.loop(0, nodes // wide)
        def _(i):
            span = pl.ds(pl.multiple_of(i * wide, wide), wide)
            weighted = src_v[:, span] * weight_ref[:, span]
            hot = one_hot(lax.broadcasted_iota(jnp.int32, (slots, wide), 0) == slot_ref[:, span])
            acc_v[...] += dot_t(hot, stacked(weighted))

        tiles = stacked(folded(jnp.transpose(acc_v[...])))
        for i in range(0, n_sub, 2):
            slot_send[:, i * LIMIT : (i + 2) * LIMIT] = folded(
                dot_t(tiles, place_v[i * LIMIT : (i + 2) * LIMIT, :])
            )

        def slot_copy(j):
            return sub_copy(5 * turn + 1, j, lanes(slot_send, sub_peer(j)), lanes(slot_recv, sub))

        def slot_wait(j):
            return sub_copy(5 * turn + 1, j, lanes(slot_send, sub_peer(j)), lanes(slot_recv, sub_from(j)))

        start_all(n_sub, slot_copy)
        slot_recv[:, own] = slot_send[:, own]

        def local(first, last):
            @pl.loop(first // 4, last // 4)
            def _(g):
                for k in range(4):
                    b = g * 4 + k
                    at = pl.multiple_of(b * BS, BS)
                    values = stacked(src_v[:, pl.ds(at, BS)])
                    high, low = split(factor_v[b])
                    half = folded(dot(values, high)) + dot(values[:SMP], low)
                    half = stacked(half)
                    ext_v[:, pl.ds(pl.multiple_of(at + halo, BS), BS)] = folded(
                        dot_t(half, high)
                    ) + dot_t(half[:SMP], low)

        if turn == 0:
            loads[1].wait()
        local(0, 32)

        if turn == 0:
            wait_all(n_sub, index_wait)

            @pl.loop(0, n_sub)
            def _(i):
                index = index_recv[i][0:1, :].astype(jnp.int32)
                rows = scatter_v.shape[0]
                span = pl.ds(pl.multiple_of(i * LIMIT, LIMIT), LIMIT)
                scatter_v[:, span] = one_hot(lax.broadcasted_iota(jnp.int32, (rows, LIMIT), 0) == index)

        if turn == 0:
            loads[2].wait()
            step_rows = 128

            @pl.loop(0, coarse_v.shape[0] // step_rows)
            def _(i):
                span = pl.ds(pl.multiple_of(i * step_rows, step_rows), step_rows)
                high, low = split(coarse_v[span, :])
                coarse_high[span, :] = high
                coarse_low[span, :] = low

        wait_all(n_sub, slot_wait)
        coarse_part = folded(dot_t(stacked(slot_recv[...]), scatter_v[...]))
        cpart[...] = coarse_part.reshape(cpart.shape)

        def reduce_sub(phase, part, recv, full, gap):
            def out(j):
                return sub_copy(phase, j, part.at[sub_peer(j)], recv.at[sub])

            def come(j):
                return sub_copy(phase, j, part.at[sub_peer(j)], recv.at[sub_from(j)])

            def share(j):
                return sub_copy(phase + 1, j, full.at[sub], full.at[sub])

            def shared(j):
                return sub_copy(phase + 1, j, full.at[sub], full.at[sub_from(j)])

            start_all(n_sub, out)
            recv[sub] = part[sub]
            local(gap, gap + 16)
            wait_all(n_sub, come)
            full[sub] = jnp.sum(recv[...], axis=0)
            start_all(n_sub, share)
            local(gap + 16, gap + 32)
            wait_all(n_sub, shared)

        def reduce_crs(phase, part, recv, full, gap):
            def out(j):
                return crs_copy(phase, j, part.at[crs_peer(j)], recv.at[crs])

            def come(j):
                return crs_copy(phase, j, part.at[crs_peer(j)], recv.at[crs_from(j)])

            def share(j):
                return crs_copy(phase + 1, j, full.at[crs], full.at[crs])

            def shared(j):
                return crs_copy(phase + 1, j, full.at[crs], full.at[crs_from(j)])

            start_all(n_crs, out)
            recv[crs] = part[crs]
            local(gap, gap + 16)
            wait_all(n_crs, come)
            full[crs] = jnp.sum(recv[...], axis=0)
            start_all(n_crs, share)
            local(gap + 16, gap + 32)
            wait_all(n_crs, shared)

        reduce_crs(4 * turn, cpart, crecv, cfull, 32)
        coarse = stacked(cfull[...].reshape(SMP, -1))
        for h in range(2):
            high = coarse_high[h * half_rows : (h + 1) * half_rows, :]
            low = coarse_low[h * half_rows : (h + 1) * half_rows, :]
            inner = folded(dot_t(coarse, high)) + dot_t(coarse[:SMP], low)
            ipart[h * 8 : (h + 1) * 8] = inner.reshape(8, 8, half_rows)

        reduce_sub(5 * turn + 2, ipart, irecv, ifull, 64)
        lifted = jnp.zeros((SMP, coarse_v.shape[1]), F32)
        for h in range(2):
            high = coarse_high[h * half_rows : (h + 1) * half_rows, :]
            low = coarse_low[h * half_rows : (h + 1) * half_rows, :]
            inner = stacked(ifull[h * 8 : (h + 1) * 8].reshape(SMP, half_rows))
            lifted = lifted + folded(dot(inner, high)) + dot(inner[:SMP], low)
        lpart[...] = lifted.reshape(lpart.shape)

        reduce_crs(4 * turn + 2, lpart, lrecv, lfull, 96)
        lifted = stacked(lfull[...].reshape(SMP, -1))
        for i in range(0, n_sub, 2):
            back_send[:, i * LIMIT : (i + 2) * LIMIT] = folded(
                dot(lifted, scatter_v[:, i * LIMIT : (i + 2) * LIMIT])
            )

        def back_copy(j):
            return sub_copy(5 * turn + 4, j, lanes(back_send, sub_peer(j)), lanes(back_recv, sub))

        def back_wait(j):
            return sub_copy(5 * turn + 4, j, lanes(back_send, sub_peer(j)), lanes(back_recv, sub_from(j)))

        start_all(n_sub, back_copy)
        back_recv[:, own] = back_send[:, own]
        if turn == 0:
            for copy in cond_copies:
                copy.wait()
            loads[8].wait()

            @pl.loop(0, blocks)
            def _(b):
                at = pl.multiple_of(b * BS, BS)
                cond = cond_v[:, pl.ds(pl.multiple_of(at + halo, BS), BS)]
                up = jnp.where(lane < BS - 1, 0.5 * (cond + pltpu.roll(cond, BS - 1, 1)), 0.0)
                down = jnp.where(lane > 0, 0.5 * (cond + pltpu.roll(cond, 1, 1)), 0.0)
                whole = kappa_ref[:, pl.ds(at, BS)] + up + down
                for k in range(4):
                    other = pl.ds(partner_ref[k * blocks + b] * BS, BS)
                    weight = 0.5 * (cond + cond_v[:, other])
                    rates_v[b, k : k + 1] = weight
                    whole = whole + weight
                rates_v[b, 4:5] = whole
                rates_v[b, 5:6] = up
                rates_v[b, 6:7] = down

        wait_all(n_sub, back_wait)
        slot_v[...] = stacked(folded(dot(stacked(back_recv[...]), place_v[...])))

        def lift(i):
            at = pl.multiple_of(i * chunk, chunk)
            span = pl.ds(at, chunk)
            hot = one_hot(lax.broadcasted_iota(jnp.int32, (slots, chunk), 0) == slot_ref[:, span])
            inside = pl.ds(pl.multiple_of(at + halo, BS), chunk)
            z = ext_v[:, inside] + weight_ref[:, span] * folded(dot(slot_v[...], hot))
            ext_v[:, inside] = z
            product = z * src_v[:, span]
            total = product[:, :BS]
            for k in range(1, chunk // BS):
                total = total + product[:, k * BS : (k + 1) * BS]
            dots_ref[2 * turn] += total

        @pl.loop(0, 2)
        def _(i):
            lift(i * (chunks - 1))

        halo_now = halo_copies(ext_v, 2 + 2 * turn)
        for copy in halo_now:
            copy.start()

        @pl.loop(1, chunks - 1)
        def _(i):
            lift(i)

        for copy in halo_now:
            copy.wait()

        per_turn = 4

        def operator(g, total):
            images = []
            for i in range(per_turn):
                b = g * per_turn + i
                v = ext_v[:, pl.ds(pl.multiple_of(b * BS + halo, BS), BS)]
                rates = rates_v[b]
                image = rates[4:5] * v
                image = image - rates[5:6] * pltpu.roll(v, BS - 1, 1)
                image = image - rates[6:7] * pltpu.roll(v, 1, 1)
                for k in range(4):
                    other = pl.ds(partner_ref[k * blocks + b] * BS, BS)
                    image = image - rates[k : k + 1] * ext_v[:, other]
                images.append(image)
                total = total + v * image
            for i in range(per_turn):
                at = pl.multiple_of((g * per_turn + i) * BS, BS)
                q_v[:, pl.ds(at, BS)] = images[i]
            return total

        dots_ref[2 * turn + 1] = lax.fori_loop(
            0, blocks // per_turn, operator, jnp.zeros((SMP, BS), F32)
        )

    apply(0, src_v, ext_one, image_one)
    apply(1, image_one, ext_two, image_two)

    kind = lax.broadcasted_iota(jnp.int32, (8, BS), 0)
    packed = jnp.zeros((8, BS), F32)
    ones = jnp.ones((8, BS), F32)
    for i in range(4):
        sums = lax.dot_general(
            ones,
            jnp.concatenate([dots_ref[i], jnp.zeros((BS - SMP, BS), F32)], axis=0),
            (((1,), (1,)), ((), ())),
            precision=lax.Precision.HIGHEST,
            preferred_element_type=F32,
        )
        packed = jnp.where(kind == i, sums, packed)
    sums_mine[...] = packed

    def sums_out(j):
        return crs_copy(8, j, sums_mine, sums_crs.at[crs])

    def sums_come(j):
        return crs_copy(8, j, sums_mine, sums_crs.at[crs_from(j)])

    def part_out(j):
        return sub_copy(10, j, sums_part, sums_sub.at[sub])

    def part_come(j):
        return sub_copy(10, j, sums_part, sums_sub.at[sub_from(j)])

    start_all(n_crs, sums_out)
    sums_crs[crs] = sums_mine[...]
    wait_all(n_crs, sums_come)
    sums_part[...] = jnp.sum(sums_crs[...], axis=0)
    start_all(n_sub, part_out)
    sums_sub[sub] = sums_part[...]
    wait_all(n_sub, part_come)
    sums = jnp.sum(sums_sub[...], axis=0)
    rz, zq, qu, ut = (sums[i : i + 1] for i in range(4))
    step = rz / zq
    rz_next = step * step * qu - rz
    ratio = rz_next / rz
    grown = 1.0 + ratio
    curvature = grown * grown * zq - 2.0 * grown * step * qu + step * step * ut
    step_next = rz_next / curvature
    near = jnp.transpose(jnp.broadcast_to(step + step_next * grown, (BS, BS)))[:SMP]
    far = jnp.transpose(jnp.broadcast_to(step * step_next, (BS, BS)))[:SMP]

    @pl.loop(0, blocks // 2)
    def _(g):
        for k in range(2):
            at = pl.multiple_of((g * 2 + k) * BS, BS)
            span = pl.ds(at, BS)
            inside = pl.ds(pl.multiple_of(at + halo, BS), BS)
            residual = src_v[:, span] - near * image_one[:, span] + far * image_two[:, span]
            image_one[:, span] = near * ext_one[:, inside] - far * ext_two[:, inside]
            image_two[:, span] = residual


def apply_call(n_sub, n_crs, src, factor, coarse_factor, real, slot, name, partner):
    nodes = src.shape[1]
    blocks = factor.shape[0]
    slots = name.shape[1] // 2
    rows, cols = coarse_factor.shape
    halo = HALO * BS
    vmem = pl.BlockSpec(memory_space=pltpu.VMEM)
    anywhere = pl.BlockSpec(memory_space=pltpu.HBM)
    wide = n_sub * LIMIT
    field = jax.ShapeDtypeStruct(src.shape, F32)
    return pl.pallas_call(
        functools.partial(apply_kernel, n_sub, n_crs),
        out_shape=(field, field),
        in_specs=[anywhere] * 6 + [pl.BlockSpec(memory_space=pltpu.SMEM)],
        out_specs=(vmem,) * 2,
        scratch_shapes=[
            pltpu.VMEM((SMP, nodes + 2 * halo), F32),
            pltpu.VMEM((SMP, nodes + 2 * halo), F32),
            pltpu.VMEM((1, nodes), F32),
            pltpu.VMEM((1, nodes), F32),
            pltpu.VMEM((1, nodes), jnp.int32),
            pltpu.VMEM((1, slots), jnp.int32),
            pltpu.VMEM((1, slots), jnp.int32),
            pltpu.VMEM((rows, cols), BF16),
            pltpu.VMEM((rows, cols), BF16),
            pltpu.VMEM((SMP, nodes), F32),
            pltpu.VMEM((blocks, BS, BS), F32),
            pltpu.VMEM((rows, cols), F32),
            pltpu.VMEM((1, nodes + 2 * halo), F32),
            pltpu.VMEM((slots, 2 * SMP), F32),
            pltpu.VMEM((wide, slots), BF16),
            pltpu.VMEM((cols, wide), BF16),
            pltpu.VMEM((n_sub, 8, LIMIT), F32),
            pltpu.VMEM((n_sub, 8, LIMIT), F32),
            pltpu.VMEM((SMP, wide), F32),
            pltpu.VMEM((SMP, wide), F32),
            pltpu.VMEM((SMP, wide), F32),
            pltpu.VMEM((SMP, wide), F32),
            pltpu.VMEM((n_crs, 8, cols), F32),
            pltpu.VMEM((n_crs, 8, cols), F32),
            pltpu.VMEM((n_crs, 8, cols), F32),
            pltpu.VMEM((n_sub, 8, rows // 2), F32),
            pltpu.VMEM((n_sub, 8, rows // 2), F32),
            pltpu.VMEM((n_sub, 8, rows // 2), F32),
            pltpu.VMEM((n_crs, 8, cols), F32),
            pltpu.VMEM((n_crs, 8, cols), F32),
            pltpu.VMEM((n_crs, 8, cols), F32),
            pltpu.VMEM((2 * SMP, slots), BF16),
            pltpu.VMEM((blocks, 8, BS), F32),
            pltpu.VMEM((4, SMP, BS), F32),
            pltpu.VMEM((8, BS), F32),
            pltpu.VMEM((n_crs, 8, BS), F32),
            pltpu.VMEM((8, BS), F32),
            pltpu.VMEM((n_sub, 8, BS), F32),
            pltpu.SemaphoreType.DMA((9,)),
            pltpu.SemaphoreType.DMA((11, n_sub)),
            pltpu.SemaphoreType.DMA((11, n_sub)),
            pltpu.SemaphoreType.DMA((9, n_crs)),
            pltpu.SemaphoreType.DMA((9, n_crs)),
            pltpu.SemaphoreType.DMA((6,)),
            pltpu.SemaphoreType.DMA((6,)),
        ],
        compiler_params=pltpu.CompilerParams(
            collective_id=0, has_side_effects=True, vmem_limit_bytes=VMEM_LIMIT * 1024 * 1024
        ),
    )(src, factor, coarse_factor, real, slot, name, partner)


def solution(mesh):
    n_sub, n_crs = mesh.shape["sub"], mesh.shape["crs"]

    def per_device(
        right_side,
        kappa_sq,
        conduct,
        partners,
        local_factor,
        restrict_weight,
        aggregate,
        owner,
        owner_coarse_row,
        coarse_factor,
    ):
        nodes = right_side.shape[1]
        slots = owner.shape[0]
        first_block = lax.axis_index(("sub", "crs")) * local_factor.shape[0] - HALO
        rest = (
            local_factor,
            coarse_factor,
            jnp.concatenate([restrict_weight, kappa_sq, conduct]).reshape(1, 3 * nodes),
            aggregate,
            jnp.concatenate([owner.reshape(slots), owner_coarse_row]).reshape(1, 2 * slots),
            (partners.T - first_block).reshape(-1),
        )
        return apply_call(n_sub, n_crs, right_side, *rest)

    return jax.shard_map(
        per_device,
        mesh=mesh,
        in_specs=(
            P(None, ("sub", "crs")),
            P(("sub", "crs")),
            P(("sub", "crs")),
            P(("sub", "crs"), None),
            P(("sub", "crs"), None, None),
            P(("sub", "crs")),
            P(("sub", "crs"), None),
            P(("sub", "crs"), None),
            P(("sub", "crs")),
            P("crs", "sub"),
        ),
        out_specs=(P(None, ("sub", "crs")), P(None, ("sub", "crs"))),
        check_vma=False,
    )
```

```python
import functools

import jax
import jax.numpy as jnp
from jax import lax
from jax.experimental import pallas as pl
from jax.experimental.pallas import tpu as pltpu
from jax.sharding import PartitionSpec as P

MESH = pl.DeviceIdType.MESH
F32 = jnp.float32
BF16 = jnp.bfloat16
HALO = 7
BS = 128
SMP = 64
LIMIT = 128
RING = 4
CORES = 2
VMEM_LIMIT = 40


def split(x):
    high = x.astype(BF16)
    return high, (x - high.astype(F32)).astype(BF16)


def dot(a, b):
    return lax.dot_general(a, b, (((1,), (0,)), ((), ())), preferred_element_type=F32)


def dot_t(a, b):
    return lax.dot_general(a, b, (((1,), (1,)), ((), ())), preferred_element_type=F32)


def stacked(x):
    return jnp.concatenate(split(x), axis=0)


def folded(y):
    half = y.shape[0] // 2
    return y[:half] + y[half:]


def farthest_first(count, depth):
    width = count // depth

    def hops(j):
        outer, inner = j // depth, j % depth
        return 2 * min(outer, width - outer) + 2 * min(inner, depth - inner) * (depth > CORES)

    return sorted(range(1, count), key=lambda j: (-hops(j), j))


def one_hot(mask):
    return jnp.where(mask, 1.0, 0.0).astype(BF16)


def apply_kernel(
    n_sub,
    n_crs,
    src_hbm,
    factor_hbm,
    coarse_hbm,
    real_hbm,
    slot_hbm,
    name_hbm,
    partner_ref,
    image_one,
    image_two,
    ext_one,
    ext_two,
    weight_ref,
    kappa_ref,
    slot_ref,
    owner_ref,
    row_ref,
    coarse_high,
    coarse_low,
    src_v,
    factor_v,
    coarse_v,
    cond_v,
    acc_v,
    place_v,
    scatter_v,
    index_send,
    index_recv,
    slot_send,
    slot_recv,
    back_send,
    back_recv,
    cpart,
    crecv,
    cfull,
    ipart,
    irecv,
    ifull,
    lpart,
    lrecv,
    lfull,
    slot_v,
    rates_v,
    dots_ref,
    sums_mine,
    sums_crs,
    sums_part,
    sums_sub,
    load_sem,
    sub_send,
    sub_recv,
    crs_send,
    crs_recv,
    halo_send,
    halo_recv,
):
    sub = lax.axis_index("sub")
    crs = lax.axis_index("crs")
    me = sub * n_crs + crs
    total = n_sub * n_crs
    right = lax.rem(me + 1, total)
    left = lax.rem(me + total - 1, total)
    nodes = src_v.shape[1]
    blocks = nodes // BS
    slots = owner_ref.shape[1]
    halo = HALO * BS

    def shifted(place, j, width, depth, sign):
        outer = lax.rem(lax.div(place, depth) + width + sign * (j // depth), width)
        inner = lax.rem(lax.rem(place, depth) + depth + sign * (j % depth), depth)
        return outer * depth + inner

    def sub_peer(j):
        return shifted(sub, j, n_sub // RING, RING, 1)

    def sub_from(j):
        return shifted(sub, j, n_sub // RING, RING, -1)

    def crs_peer(j):
        return shifted(crs, j, n_crs // CORES, CORES, 1)

    def crs_from(j):
        return shifted(crs, j, n_crs // CORES, CORES, -1)

    def at_device(d):
        return (d // n_crs, lax.rem(d, n_crs))

    def sub_copy(phase, j, source, target):
        return pltpu.make_async_remote_copy(
            src_ref=source,
            dst_ref=target,
            send_sem=sub_send.at[phase, j],
            recv_sem=sub_recv.at[phase, j],
            device_id=(sub_peer(j), crs),
            device_id_type=MESH,
        )

    def crs_copy(phase, j, source, target):
        return pltpu.make_async_remote_copy(
            src_ref=source,
            dst_ref=target,
            send_sem=crs_send.at[phase, j],
            recv_sem=crs_recv.at[phase, j],
            device_id=(sub, crs_peer(j)),
            device_id_type=MESH,
        )

    def lanes(ref, i):
        return ref.at[:, pl.ds(pl.multiple_of(i * LIMIT, LIMIT), LIMIT)]

    def start_all(count, copy):
        for j in farthest_first(count, RING if count == n_sub else CORES):
            copy(j).start()

    def wait_all(count, copy):
        @pl.loop(1, count)
        def _(j):
            copy(j).wait()

    loads = [
        pltpu.make_async_copy(src_hbm, src_v, load_sem.at[0]),
        pltpu.make_async_copy(factor_hbm, factor_v, load_sem.at[1]),
        pltpu.make_async_copy(coarse_hbm, coarse_v, load_sem.at[2]),
        pltpu.make_async_copy(real_hbm.at[:, pl.ds(0, nodes)], weight_ref, load_sem.at[3]),
        pltpu.make_async_copy(slot_hbm, slot_ref, load_sem.at[4]),
        pltpu.make_async_copy(name_hbm.at[:, pl.ds(0, slots)], owner_ref, load_sem.at[5]),
        pltpu.make_async_copy(name_hbm.at[:, pl.ds(slots, slots)], row_ref, load_sem.at[6]),
        pltpu.make_async_copy(
            real_hbm.at[:, pl.ds(2 * nodes, nodes)],
            cond_v.at[:, pl.ds(halo, nodes)],
            load_sem.at[7],
        ),
        pltpu.make_async_copy(real_hbm.at[:, pl.ds(nodes, nodes)], kappa_ref, load_sem.at[8]),
    ]
    for i in (5, 6, 7, 3, 4, 0, 8, 1, 2):
        loads[i].start()

    barrier = pltpu.get_barrier_semaphore()

    @pl.loop(1, n_sub)
    def _(j):
        pl.semaphore_signal(barrier, inc=1, device_id=(sub_peer(j), crs), device_id_type=MESH)

    @pl.loop(1, n_crs)
    def _(j):
        pl.semaphore_signal(barrier, inc=1, device_id=(sub, crs_peer(j)), device_id_type=MESH)

    pl.semaphore_signal(barrier, inc=1, device_id=at_device(left), device_id_type=MESH)
    pl.semaphore_signal(barrier, inc=1, device_id=at_device(right), device_id_type=MESH)

    loads[5].wait()
    loads[6].wait()
    owner_row = owner_ref[...]
    group = lax.broadcasted_iota(jnp.int32, (n_sub, slots), 0)
    members = jnp.where(owner_row == group, 1.0, 0.0)
    before = one_hot(
        lax.broadcasted_iota(jnp.int32, (slots, slots), 0)
        < lax.broadcasted_iota(jnp.int32, (slots, slots), 1)
    )
    ahead = dot(members.astype(BF16), before)
    rank = jnp.sum(members * ahead, axis=0, keepdims=True)
    place = owner_row * LIMIT + rank.astype(jnp.int32)
    row_one = stacked(jnp.broadcast_to((row_ref[...] + 1).astype(F32), (8, slots)))

    wide = 2048
    lists = n_sub * wide // nodes

    def list_slots(i):
        start = pl.multiple_of(i * lists * LIMIT, lists * LIMIT)
        hot = one_hot(
            lax.broadcasted_iota(jnp.int32, (lists * LIMIT, slots), 0) + start == place
        )
        place_v[pl.ds(start, lists * LIMIT), :] = hot
        index = folded(dot_t(row_one, hot)) - 1.0
        for k in range(lists):
            index_send[i * lists + k] = index[:, k * LIMIT : (k + 1) * LIMIT]

    def index_copy(j):
        return sub_copy(0, j, index_send.at[sub_peer(j)], index_recv.at[sub])

    def index_wait(j):
        return sub_copy(0, j, index_send.at[sub_peer(j)], index_recv.at[sub_from(j)])

    def halo_copies(buffer, phase):
        up = pltpu.make_async_remote_copy(
            src_ref=buffer.at[:, pl.ds(nodes, halo)],
            dst_ref=buffer.at[:, pl.ds(0, halo)],
            send_sem=halo_send.at[phase],
            recv_sem=halo_recv.at[phase],
            device_id=at_device(right),
            device_id_type=MESH,
        )
        down = pltpu.make_async_remote_copy(
            src_ref=buffer.at[:, pl.ds(halo, halo)],
            dst_ref=buffer.at[:, pl.ds(halo + nodes, halo)],
            send_sem=halo_send.at[phase + 1],
            recv_sem=halo_recv.at[phase + 1],
            device_id=at_device(left),
            device_id_type=MESH,
        )
        return up, down

    cond_copies = halo_copies(cond_v, 0)

    half_rows = coarse_v.shape[0] // 2
    own = pl.ds(pl.multiple_of(sub * LIMIT, LIMIT), LIMIT)
    chunk = 1024
    chunks = nodes // chunk
    lane = lax.broadcasted_iota(jnp.int32, (1, BS), 1)
    dots_ref[...] = jnp.zeros_like(dots_ref)

    def restrict(values, i):
        span = pl.ds(pl.multiple_of(i * wide, wide), wide)
        weighted = stacked(values[:, span] * weight_ref[:, span])
        hot = one_hot(lax.broadcasted_iota(jnp.int32, (slots, wide), 0) == slot_ref[:, span])
        acc_v[...] += dot_t(hot, weighted)

    def apply(turn, src_v, ext_v, q_v):
        if turn == 0:
            loads[3].wait()
            loads[4].wait()
            loads[0].wait()
        if turn == 0:
            acc_v[...] = jnp.zeros_like(acc_v)

            @pl.loop(0, nodes // wide)
            def _(i):
                restrict(src_v, i)
                list_slots(i)

            index_recv[sub] = index_send[sub]
            loads[7].wait()
            pl.semaphore_wait(barrier, n_sub + n_crs)
            start_all(n_sub, index_copy)

        tiles = stacked(folded(jnp.transpose(acc_v[...])))
        for i in range(0, n_sub, 2):
            slot_send[:, i * LIMIT : (i + 2) * LIMIT] = folded(
                dot_t(tiles, place_v[i * LIMIT : (i + 2) * LIMIT, :])
            )

        def slot_copy(j):
            return sub_copy(5 * turn + 1, j, lanes(slot_send, sub_peer(j)), lanes(slot_recv, sub))

        def slot_wait(j):
            return sub_copy(5 * turn + 1, j, lanes(slot_send, sub_peer(j)), lanes(slot_recv, sub_from(j)))

        start_all(n_sub, slot_copy)
        if turn == 0:
            for copy in cond_copies:
                copy.start()
        slot_recv[:, own] = slot_send[:, own]

        def local(first, last):
            @pl.loop(first // 4, last // 4)
            def _(g):
                for k in range(4):
                    b = g * 4 + k
                    at = pl.multiple_of(b * BS, BS)
                    values = stacked(src_v[:, pl.ds(at, BS)])
                    high, low = split(factor_v[b])
                    half = folded(dot(values, high)) + dot(values[:SMP], low)
                    half = stacked(half)
                    ext_v[:, pl.ds(pl.multiple_of(at + halo, BS), BS)] = folded(
                        dot_t(half, high)
                    ) + dot_t(half[:SMP], low)

        if turn == 0:
            loads[1].wait()
        local(0, 32)

        if turn == 0:
            wait_all(n_sub, index_wait)

            @pl.loop(0, n_sub)
            def _(i):
                index = index_recv[i][0:1, :].astype(jnp.int32)
                rows = scatter_v.shape[0]
                span = pl.ds(pl.multiple_of(i * LIMIT, LIMIT), LIMIT)
                scatter_v[:, span] = one_hot(lax.broadcasted_iota(jnp.int32, (rows, LIMIT), 0) == index)

        if turn == 0:
            loads[2].wait()
            step_rows = 128

            @pl.loop(0, coarse_v.shape[0] // step_rows)
            def _(i):
                span = pl.ds(pl.multiple_of(i * step_rows, step_rows), step_rows)
                high, low = split(coarse_v[span, :])
                coarse_high[span, :] = high
                coarse_low[span, :] = low

        wait_all(n_sub, slot_wait)
        coarse_part = folded(dot_t(stacked(slot_recv[...]), scatter_v[...]))
        cpart[...] = coarse_part.reshape(cpart.shape)

        def reduce_sub(phase, part, recv, full, gap):
            def out(j):
                return sub_copy(phase, j, part.at[sub_peer(j)], recv.at[sub])

            def come(j):
                return sub_copy(phase, j, part.at[sub_peer(j)], recv.at[sub_from(j)])

            def share(j):
                return sub_copy(phase + 1, j, full.at[sub], full.at[sub])

            def shared(j):
                return sub_copy(phase + 1, j, full.at[sub], full.at[sub_from(j)])

            start_all(n_sub, out)
            recv[sub] = part[sub]
            local(gap, gap + 16)
            wait_all(n_sub, come)
            full[sub] = jnp.sum(recv[...], axis=0)
            start_all(n_sub, share)
            local(gap + 16, gap + 32)
            wait_all(n_sub, shared)

        def reduce_crs(phase, part, recv, full, gap):
            def out(j):
                return crs_copy(phase, j, part.at[crs_peer(j)], recv.at[crs])

            def come(j):
                return crs_copy(phase, j, part.at[crs_peer(j)], recv.at[crs_from(j)])

            def share(j):
                return crs_copy(phase + 1, j, full.at[crs], full.at[crs])

            def shared(j):
                return crs_copy(phase + 1, j, full.at[crs], full.at[crs_from(j)])

            start_all(n_crs, out)
            recv[crs] = part[crs]
            local(gap, gap + 16)
            wait_all(n_crs, come)
            full[crs] = jnp.sum(recv[...], axis=0)
            start_all(n_crs, share)
            local(gap + 16, gap + 32)
            wait_all(n_crs, shared)

        reduce_crs(4 * turn, cpart, crecv, cfull, 32)
        coarse = stacked(cfull[...].reshape(SMP, -1))
        for h in range(2):
            high = coarse_high[h * half_rows : (h + 1) * half_rows, :]
            low = coarse_low[h * half_rows : (h + 1) * half_rows, :]
            inner = folded(dot_t(coarse, high)) + dot_t(coarse[:SMP], low)
            ipart[h * 8 : (h + 1) * 8] = inner.reshape(8, 8, half_rows)

        reduce_sub(5 * turn + 2, ipart, irecv, ifull, 64)
        lifted = jnp.zeros((SMP, coarse_v.shape[1]), F32)
        for h in range(2):
            high = coarse_high[h * half_rows : (h + 1) * half_rows, :]
            low = coarse_low[h * half_rows : (h + 1) * half_rows, :]
            inner = stacked(ifull[h * 8 : (h + 1) * 8].reshape(SMP, half_rows))
            lifted = lifted + folded(dot(inner, high)) + dot(inner[:SMP], low)
        lpart[...] = lifted.reshape(lpart.shape)

        reduce_crs(4 * turn + 2, lpart, lrecv, lfull, 96)
        lifted = stacked(lfull[...].reshape(SMP, -1))
        for i in range(0, n_sub, 2):
            back_send[:, i * LIMIT : (i + 2) * LIMIT] = folded(
                dot(lifted, scatter_v[:, i * LIMIT : (i + 2) * LIMIT])
            )

        def back_copy(j):
            return sub_copy(5 * turn + 4, j, lanes(back_send, sub_peer(j)), lanes(back_recv, sub))

        def back_wait(j):
            return sub_copy(5 * turn + 4, j, lanes(back_send, sub_peer(j)), lanes(back_recv, sub_from(j)))

        start_all(n_sub, back_copy)
        back_recv[:, own] = back_send[:, own]
        if turn == 0:
            for copy in cond_copies:
                copy.wait()
            loads[8].wait()

            @pl.loop(0, blocks)
            def _(b):
                at = pl.multiple_of(b * BS, BS)
                cond = cond_v[:, pl.ds(pl.multiple_of(at + halo, BS), BS)]
                up = jnp.where(lane < BS - 1, 0.5 * (cond + pltpu.roll(cond, BS - 1, 1)), 0.0)
                down = jnp.where(lane > 0, 0.5 * (cond + pltpu.roll(cond, 1, 1)), 0.0)
                whole = kappa_ref[:, pl.ds(at, BS)] + up + down
                for k in range(4):
                    other = pl.ds(partner_ref[k * blocks + b] * BS, BS)
                    weight = 0.5 * (cond + cond_v[:, other])
                    rates_v[b, k : k + 1] = weight
                    whole = whole + weight
                rates_v[b, 4:5] = whole
                rates_v[b, 5:6] = up
                rates_v[b, 6:7] = down

        wait_all(n_sub, back_wait)
        slot_v[...] = stacked(folded(dot(stacked(back_recv[...]), place_v[...])))

        def lift(i):
            at = pl.multiple_of(i * chunk, chunk)
            span = pl.ds(at, chunk)
            hot = one_hot(lax.broadcasted_iota(jnp.int32, (slots, chunk), 0) == slot_ref[:, span])
            inside = pl.ds(pl.multiple_of(at + halo, BS), chunk)
            z = ext_v[:, inside] + weight_ref[:, span] * folded(dot(slot_v[...], hot))
            ext_v[:, inside] = z
            product = z * src_v[:, span]
            total = product[:, :BS]
            for k in range(1, chunk // BS):
                total = total + product[:, k * BS : (k + 1) * BS]
            dots_ref[2 * turn] += total

        @pl.loop(0, 2)
        def _(i):
            lift(i * (chunks - 1))

        halo_now = halo_copies(ext_v, 2 + 2 * turn)
        for copy in halo_now:
            copy.start()

        @pl.loop(1, chunks - 1)
        def _(i):
            lift(i)

        for copy in halo_now:
            copy.wait()

        per_turn = 4

        def operator(g, total):
            images = []
            for i in range(per_turn):
                b = g * per_turn + i
                v = ext_v[:, pl.ds(pl.multiple_of(b * BS + halo, BS), BS)]
                rates = rates_v[b]
                image = rates[4:5] * v
                image = image - rates[5:6] * pltpu.roll(v, BS - 1, 1)
                image = image - rates[6:7] * pltpu.roll(v, 1, 1)
                for k in range(4):
                    other = pl.ds(partner_ref[k * blocks + b] * BS, BS)
                    image = image - rates[k : k + 1] * ext_v[:, other]
                images.append(image)
                total = total + v * image
            for i in range(per_turn):
                at = pl.multiple_of((g * per_turn + i) * BS, BS)
                q_v[:, pl.ds(at, BS)] = images[i]
            return total

        zero = jnp.zeros((SMP, BS), F32)
        if turn == 0:
            groups = wide // BS // per_turn

            def operate(i, total):
                for g in range(groups):
                    total = operator(i * groups + g, total)
                return total

            def both(i, total):
                restrict(q_v, i - 1)
                return operate(i, total)

            acc_v[...] = jnp.zeros_like(acc_v)
            first = operate(0, zero)
            dots_ref[1] = lax.fori_loop(1, nodes // wide, both, first)
            restrict(q_v, nodes // wide - 1)
        else:
            dots_ref[3] = lax.fori_loop(0, blocks // per_turn, operator, zero)

    apply(0, src_v, ext_one, image_one)
    apply(1, image_one, ext_two, image_two)

    kind = lax.broadcasted_iota(jnp.int32, (8, BS), 0)
    packed = jnp.zeros((8, BS), F32)
    ones = jnp.ones((8, BS), F32)
    for i in range(4):
        sums = lax.dot_general(
            ones,
            jnp.concatenate([dots_ref[i], jnp.zeros((BS - SMP, BS), F32)], axis=0),
            (((1,), (1,)), ((), ())),
            precision=lax.Precision.HIGHEST,
            preferred_element_type=F32,
        )
        packed = jnp.where(kind == i, sums, packed)
    sums_mine[...] = packed

    def sums_out(j):
        return crs_copy(8, j, sums_mine, sums_crs.at[crs])

    def sums_come(j):
        return crs_copy(8, j, sums_mine, sums_crs.at[crs_from(j)])

    def part_out(j):
        return sub_copy(10, j, sums_part, sums_sub.at[sub])

    def part_come(j):
        return sub_copy(10, j, sums_part, sums_sub.at[sub_from(j)])

    start_all(n_crs, sums_out)
    sums_crs[crs] = sums_mine[...]
    wait_all(n_crs, sums_come)
    sums_part[...] = jnp.sum(sums_crs[...], axis=0)
    start_all(n_sub, part_out)
    sums_sub[sub] = sums_part[...]
    wait_all(n_sub, part_come)
    sums = jnp.sum(sums_sub[...], axis=0)
    rz, zq, qu, ut = (sums[i : i + 1] for i in range(4))
    step = rz / zq
    rz_next = step * step * qu - rz
    ratio = rz_next / rz
    grown = 1.0 + ratio
    curvature = grown * grown * zq - 2.0 * grown * step * qu + step * step * ut
    step_next = rz_next / curvature
    near = jnp.transpose(jnp.broadcast_to(step + step_next * grown, (BS, BS)))[:SMP]
    far = jnp.transpose(jnp.broadcast_to(step * step_next, (BS, BS)))[:SMP]

    @pl.loop(0, blocks // 2)
    def _(g):
        for k in range(2):
            at = pl.multiple_of((g * 2 + k) * BS, BS)
            span = pl.ds(at, BS)
            inside = pl.ds(pl.multiple_of(at + halo, BS), BS)
            residual = src_v[:, span] - near * image_one[:, span] + far * image_two[:, span]
            image_one[:, span] = near * ext_one[:, inside] - far * ext_two[:, inside]
            image_two[:, span] = residual


def apply_call(n_sub, n_crs, src, factor, coarse_factor, real, slot, name, partner):
    nodes = src.shape[1]
    blocks = factor.shape[0]
    slots = name.shape[1] // 2
    rows, cols = coarse_factor.shape
    halo = HALO * BS
    vmem = pl.BlockSpec(memory_space=pltpu.VMEM)
    anywhere = pl.BlockSpec(memory_space=pltpu.HBM)
    wide = n_sub * LIMIT
    field = jax.ShapeDtypeStruct(src.shape, F32)
    return pl.pallas_call(
        functools.partial(apply_kernel, n_sub, n_crs),
        out_shape=(field, field),
        in_specs=[anywhere] * 6 + [pl.BlockSpec(memory_space=pltpu.SMEM)],
        out_specs=(vmem,) * 2,
        scratch_shapes=[
            pltpu.VMEM((SMP, nodes + 2 * halo), F32),
            pltpu.VMEM((SMP, nodes + 2 * halo), F32),
            pltpu.VMEM((1, nodes), F32),
            pltpu.VMEM((1, nodes), F32),
            pltpu.VMEM((1, nodes), jnp.int32),
            pltpu.VMEM((1, slots), jnp.int32),
            pltpu.VMEM((1, slots), jnp.int32),
            pltpu.VMEM((rows, cols), BF16),
            pltpu.VMEM((rows, cols), BF16),
            pltpu.VMEM((SMP, nodes), F32),
            pltpu.VMEM((blocks, BS, BS), F32),
            pltpu.VMEM((rows, cols), F32),
            pltpu.VMEM((1, nodes + 2 * halo), F32),
            pltpu.VMEM((slots, 2 * SMP), F32),
            pltpu.VMEM((wide, slots), BF16),
            pltpu.VMEM((cols, wide), BF16),
            pltpu.VMEM((n_sub, 8, LIMIT), F32),
            pltpu.VMEM((n_sub, 8, LIMIT), F32),
            pltpu.VMEM((SMP, wide), F32),
            pltpu.VMEM((SMP, wide), F32),
            pltpu.VMEM((SMP, wide), F32),
            pltpu.VMEM((SMP, wide), F32),
            pltpu.VMEM((n_crs, 8, cols), F32),
            pltpu.VMEM((n_crs, 8, cols), F32),
            pltpu.VMEM((n_crs, 8, cols), F32),
            pltpu.VMEM((n_sub, 8, rows // 2), F32),
            pltpu.VMEM((n_sub, 8, rows // 2), F32),
            pltpu.VMEM((n_sub, 8, rows // 2), F32),
            pltpu.VMEM((n_crs, 8, cols), F32),
            pltpu.VMEM((n_crs, 8, cols), F32),
            pltpu.VMEM((n_crs, 8, cols), F32),
            pltpu.VMEM((2 * SMP, slots), BF16),
            pltpu.VMEM((blocks, 8, BS), F32),
            pltpu.VMEM((4, SMP, BS), F32),
            pltpu.VMEM((8, BS), F32),
            pltpu.VMEM((n_crs, 8, BS), F32),
            pltpu.VMEM((8, BS), F32),
            pltpu.VMEM((n_sub, 8, BS), F32),
            pltpu.SemaphoreType.DMA((9,)),
            pltpu.SemaphoreType.DMA((11, n_sub)),
            pltpu.SemaphoreType.DMA((11, n_sub)),
            pltpu.SemaphoreType.DMA((9, n_crs)),
            pltpu.SemaphoreType.DMA((9, n_crs)),
            pltpu.SemaphoreType.DMA((6,)),
            pltpu.SemaphoreType.DMA((6,)),
        ],
        compiler_params=pltpu.CompilerParams(
            collective_id=0, has_side_effects=True, vmem_limit_bytes=VMEM_LIMIT * 1024 * 1024
        ),
    )(src, factor, coarse_factor, real, slot, name, partner)


def solution(mesh):
    n_sub, n_crs = mesh.shape["sub"], mesh.shape["crs"]

    def per_device(
        right_side,
        kappa_sq,
        conduct,
        partners,
        local_factor,
        restrict_weight,
        aggregate,
        owner,
        owner_coarse_row,
        coarse_factor,
    ):
        nodes = right_side.shape[1]
        slots = owner.shape[0]
        first_block = lax.axis_index(("sub", "crs")) * local_factor.shape[0] - HALO
        rest = (
            local_factor,
            coarse_factor,
            jnp.concatenate([restrict_weight, kappa_sq, conduct]).reshape(1, 3 * nodes),
            aggregate,
            jnp.concatenate([owner.reshape(slots), owner_coarse_row]).reshape(1, 2 * slots),
            (partners.T - first_block).reshape(-1),
        )
        return apply_call(n_sub, n_crs, right_side, *rest)

    return jax.shard_map(
        per_device,
        mesh=mesh,
        in_specs=(
            P(None, ("sub", "crs")),
            P(("sub", "crs")),
            P(("sub", "crs")),
            P(("sub", "crs"), None),
            P(("sub", "crs"), None, None),
            P(("sub", "crs")),
            P(("sub", "crs"), None),
            P(("sub", "crs"), None),
            P(("sub", "crs")),
            P("crs", "sub"),
        ),
        out_specs=(P(None, ("sub", "crs")), P(None, ("sub", "crs"))),
        check_vma=False,
    )
```

```python
import functools

import jax
import jax.numpy as jnp
from jax import lax
from jax.experimental import pallas as pl
from jax.experimental.pallas import tpu as pltpu
from jax.sharding import PartitionSpec as P

MESH = pl.DeviceIdType.MESH
F32 = jnp.float32
BF16 = jnp.bfloat16
HALO = 7
BS = 128
SMP = 64
LIMIT = 128
RING = 4
CORES = 2
VMEM_LIMIT = 40


def split(x):
    high = x.astype(BF16)
    return high, (x - high.astype(F32)).astype(BF16)


def dot(a, b):
    return lax.dot_general(a, b, (((1,), (0,)), ((), ())), preferred_element_type=F32)


def dot_t(a, b):
    return lax.dot_general(a, b, (((1,), (1,)), ((), ())), preferred_element_type=F32)


def stacked(x):
    return jnp.concatenate(split(x), axis=0)


def folded(y):
    half = y.shape[0] // 2
    return y[:half] + y[half:]


def farthest_first(count, depth):
    width = count // depth

    def hops(j):
        outer, inner = j // depth, j % depth
        return 2 * min(outer, width - outer) + 2 * min(inner, depth - inner) * (depth > CORES)

    return sorted(range(1, count), key=lambda j: (-hops(j), j))


def one_hot(mask):
    return jnp.where(mask, 1.0, 0.0).astype(BF16)


def apply_kernel(
    n_sub,
    n_crs,
    src_hbm,
    factor_hbm,
    coarse_hbm,
    real_hbm,
    name_hbm,
    partner_ref,
    image_one,
    image_two,
    ext_one,
    ext_two,
    weight_ref,
    kappa_ref,
    slot_ref,
    owner_ref,
    row_ref,
    coarse_high,
    coarse_low,
    src_v,
    factor_v,
    coarse_v,
    cond_v,
    acc_v,
    place_v,
    scatter_v,
    index_send,
    index_recv,
    slot_send,
    slot_recv,
    back_send,
    back_recv,
    cpart,
    crecv,
    cfull,
    ipart,
    irecv,
    ifull,
    lpart,
    lrecv,
    lfull,
    slot_v,
    rates_v,
    dots_ref,
    sums_mine,
    sums_crs,
    sums_part,
    sums_sub,
    load_sem,
    sub_send,
    sub_recv,
    crs_send,
    crs_recv,
    halo_send,
    halo_recv,
):
    sub = lax.axis_index("sub")
    crs = lax.axis_index("crs")
    me = sub * n_crs + crs
    total = n_sub * n_crs
    right = lax.rem(me + 1, total)
    left = lax.rem(me + total - 1, total)
    nodes = src_v.shape[1]
    blocks = nodes // BS
    slots = owner_ref.shape[1]
    halo = HALO * BS

    def shifted(place, j, width, depth, sign):
        outer = lax.rem(lax.div(place, depth) + width + sign * (j // depth), width)
        inner = lax.rem(lax.rem(place, depth) + depth + sign * (j % depth), depth)
        return outer * depth + inner

    def sub_peer(j):
        return shifted(sub, j, n_sub // RING, RING, 1)

    def sub_from(j):
        return shifted(sub, j, n_sub // RING, RING, -1)

    def crs_peer(j):
        return shifted(crs, j, n_crs // CORES, CORES, 1)

    def crs_from(j):
        return shifted(crs, j, n_crs // CORES, CORES, -1)

    def at_device(d):
        return (d // n_crs, lax.rem(d, n_crs))

    def sub_copy(phase, j, source, target):
        return pltpu.make_async_remote_copy(
            src_ref=source,
            dst_ref=target,
            send_sem=sub_send.at[phase, j],
            recv_sem=sub_recv.at[phase, j],
            device_id=(sub_peer(j), crs),
            device_id_type=MESH,
        )

    def crs_copy(phase, j, source, target):
        return pltpu.make_async_remote_copy(
            src_ref=source,
            dst_ref=target,
            send_sem=crs_send.at[phase, j],
            recv_sem=crs_recv.at[phase, j],
            device_id=(sub, crs_peer(j)),
            device_id_type=MESH,
        )

    def lanes(ref, i):
        return ref.at[:, pl.ds(pl.multiple_of(i * LIMIT, LIMIT), LIMIT)]

    def start_all(count, copy):
        for j in farthest_first(count, RING if count == n_sub else CORES):
            copy(j).start()

    def wait_all(count, copy):
        @pl.loop(1, count)
        def _(j):
            copy(j).wait()

    loads = [
        pltpu.make_async_copy(src_hbm, src_v, load_sem.at[0]),
        pltpu.make_async_copy(factor_hbm, factor_v, load_sem.at[1]),
        pltpu.make_async_copy(coarse_hbm, coarse_v, load_sem.at[2]),
        pltpu.make_async_copy(real_hbm.at[:, pl.ds(0, nodes)], weight_ref, load_sem.at[3]),
        pltpu.make_async_copy(real_hbm.at[:, pl.ds(3 * nodes, nodes)], slot_ref, load_sem.at[4]),
        pltpu.make_async_copy(name_hbm.at[:, pl.ds(0, slots)], owner_ref, load_sem.at[5]),
        pltpu.make_async_copy(name_hbm.at[:, pl.ds(slots, slots)], row_ref, load_sem.at[6]),
        pltpu.make_async_copy(
            real_hbm.at[:, pl.ds(2 * nodes, nodes)],
            cond_v.at[:, pl.ds(halo, nodes)],
            load_sem.at[7],
        ),
        pltpu.make_async_copy(real_hbm.at[:, pl.ds(nodes, nodes)], kappa_ref, load_sem.at[8]),
    ]
    for i in (5, 6, 7, 3, 4, 0, 8, 1, 2):
        loads[i].start()

    barrier = pltpu.get_barrier_semaphore()

    @pl.loop(1, n_sub)
    def _(j):
        pl.semaphore_signal(barrier, inc=1, device_id=(sub_peer(j), crs), device_id_type=MESH)

    @pl.loop(1, n_crs)
    def _(j):
        pl.semaphore_signal(barrier, inc=1, device_id=(sub, crs_peer(j)), device_id_type=MESH)

    pl.semaphore_signal(barrier, inc=1, device_id=at_device(left), device_id_type=MESH)
    pl.semaphore_signal(barrier, inc=1, device_id=at_device(right), device_id_type=MESH)

    loads[5].wait()
    loads[6].wait()
    owner_row = owner_ref[...]
    group = lax.broadcasted_iota(jnp.int32, (n_sub, slots), 0)
    members = jnp.where(owner_row == group, 1.0, 0.0)
    before = one_hot(
        lax.broadcasted_iota(jnp.int32, (slots, slots), 0)
        < lax.broadcasted_iota(jnp.int32, (slots, slots), 1)
    )
    ahead = dot(members.astype(BF16), before)
    rank = jnp.sum(members * ahead, axis=0, keepdims=True)
    place = owner_row * LIMIT + rank.astype(jnp.int32)
    row_one = stacked(jnp.broadcast_to((row_ref[...] + 1).astype(F32), (8, slots)))

    wide = 2048
    lists = n_sub * wide // nodes

    def list_slots(i):
        start = pl.multiple_of(i * lists * LIMIT, lists * LIMIT)
        hot = one_hot(
            lax.broadcasted_iota(jnp.int32, (lists * LIMIT, slots), 0) + start == place
        )
        place_v[pl.ds(start, lists * LIMIT), :] = hot
        index = folded(dot_t(row_one, hot)) - 1.0
        for k in range(lists):
            index_send[i * lists + k] = index[:, k * LIMIT : (k + 1) * LIMIT]

    def index_copy(j):
        return sub_copy(0, j, index_send.at[sub_peer(j)], index_recv.at[sub])

    def index_wait(j):
        return sub_copy(0, j, index_send.at[sub_peer(j)], index_recv.at[sub_from(j)])

    def halo_copies(buffer, phase):
        up = pltpu.make_async_remote_copy(
            src_ref=buffer.at[:, pl.ds(nodes, halo)],
            dst_ref=buffer.at[:, pl.ds(0, halo)],
            send_sem=halo_send.at[phase],
            recv_sem=halo_recv.at[phase],
            device_id=at_device(right),
            device_id_type=MESH,
        )
        down = pltpu.make_async_remote_copy(
            src_ref=buffer.at[:, pl.ds(halo, halo)],
            dst_ref=buffer.at[:, pl.ds(halo + nodes, halo)],
            send_sem=halo_send.at[phase + 1],
            recv_sem=halo_recv.at[phase + 1],
            device_id=at_device(left),
            device_id_type=MESH,
        )
        return up, down

    cond_copies = halo_copies(cond_v, 0)

    half_rows = coarse_v.shape[0] // 2
    own = pl.ds(pl.multiple_of(sub * LIMIT, LIMIT), LIMIT)
    chunk = 1024
    chunks = nodes // chunk
    lane = lax.broadcasted_iota(jnp.int32, (1, BS), 1)
    dots_ref[...] = jnp.zeros_like(dots_ref)

    def restrict(values, i):
        span = pl.ds(pl.multiple_of(i * wide, wide), wide)
        weighted = stacked(values[:, span] * weight_ref[:, span])
        hot = one_hot(lax.broadcasted_iota(jnp.int32, (slots, wide), 0) == slot_ref[:, span].astype(jnp.int32))
        acc_v[...] += dot_t(hot, weighted)

    def apply(turn, src_v, ext_v, q_v):
        if turn == 0:
            loads[3].wait()
            loads[4].wait()
            loads[0].wait()
        if turn == 0:
            acc_v[...] = jnp.zeros_like(acc_v)

            @pl.loop(0, nodes // wide)
            def _(i):
                restrict(src_v, i)
                list_slots(i)

            index_recv[sub] = index_send[sub]
            loads[7].wait()
            pl.semaphore_wait(barrier, n_sub + n_crs)
            start_all(n_sub, index_copy)

        tiles = stacked(folded(jnp.transpose(acc_v[...])))
        for i in range(0, n_sub, 2):
            slot_send[:, i * LIMIT : (i + 2) * LIMIT] = folded(
                dot_t(tiles, place_v[i * LIMIT : (i + 2) * LIMIT, :])
            )

        def slot_copy(j):
            return sub_copy(5 * turn + 1, j, lanes(slot_send, sub_peer(j)), lanes(slot_recv, sub))

        def slot_wait(j):
            return sub_copy(5 * turn + 1, j, lanes(slot_send, sub_peer(j)), lanes(slot_recv, sub_from(j)))

        start_all(n_sub, slot_copy)
        if turn == 0:
            for copy in cond_copies:
                copy.start()
        slot_recv[:, own] = slot_send[:, own]

        def local(first, last):
            @pl.loop(first // 4, last // 4)
            def _(g):
                for k in range(4):
                    b = g * 4 + k
                    at = pl.multiple_of(b * BS, BS)
                    values = stacked(src_v[:, pl.ds(at, BS)])
                    high, low = split(factor_v[b])
                    half = folded(dot(values, high)) + dot(values[:SMP], low)
                    half = stacked(half)
                    ext_v[:, pl.ds(pl.multiple_of(at + halo, BS), BS)] = folded(
                        dot_t(half, high)
                    ) + dot_t(half[:SMP], low)

        if turn == 0:
            loads[1].wait()
        local(0, 32)

        if turn == 0:
            wait_all(n_sub, index_wait)

            @pl.loop(0, n_sub)
            def _(i):
                index = index_recv[i][0:1, :].astype(jnp.int32)
                rows = scatter_v.shape[0]
                span = pl.ds(pl.multiple_of(i * LIMIT, LIMIT), LIMIT)
                scatter_v[:, span] = one_hot(lax.broadcasted_iota(jnp.int32, (rows, LIMIT), 0) == index)

        if turn == 0:
            loads[2].wait()
            step_rows = 128

            @pl.loop(0, coarse_v.shape[0] // step_rows)
            def _(i):
                span = pl.ds(pl.multiple_of(i * step_rows, step_rows), step_rows)
                high, low = split(coarse_v[span, :])
                coarse_high[span, :] = high
                coarse_low[span, :] = low

        wait_all(n_sub, slot_wait)
        coarse_part = folded(dot_t(stacked(slot_recv[...]), scatter_v[...]))
        cpart[...] = coarse_part.reshape(cpart.shape)

        def reduce_sub(phase, part, recv, full, gap):
            def out(j):
                return sub_copy(phase, j, part.at[sub_peer(j)], recv.at[sub])

            def come(j):
                return sub_copy(phase, j, part.at[sub_peer(j)], recv.at[sub_from(j)])

            def share(j):
                return sub_copy(phase + 1, j, full.at[sub], full.at[sub])

            def shared(j):
                return sub_copy(phase + 1, j, full.at[sub], full.at[sub_from(j)])

            start_all(n_sub, out)
            recv[sub] = part[sub]
            local(gap, gap + 16)
            wait_all(n_sub, come)
            full[sub] = jnp.sum(recv[...], axis=0)
            start_all(n_sub, share)
            local(gap + 16, gap + 32)
            wait_all(n_sub, shared)

        def reduce_crs(phase, part, recv, full, gap):
            def out(j):
                return crs_copy(phase, j, part.at[crs_peer(j)], recv.at[crs])

            def come(j):
                return crs_copy(phase, j, part.at[crs_peer(j)], recv.at[crs_from(j)])

            def share(j):
                return crs_copy(phase + 1, j, full.at[crs], full.at[crs])

            def shared(j):
                return crs_copy(phase + 1, j, full.at[crs], full.at[crs_from(j)])

            start_all(n_crs, out)
            recv[crs] = part[crs]
            local(gap, gap + 16)
            wait_all(n_crs, come)
            full[crs] = jnp.sum(recv[...], axis=0)
            start_all(n_crs, share)
            local(gap + 16, gap + 32)
            wait_all(n_crs, shared)

        reduce_crs(4 * turn, cpart, crecv, cfull, 32)
        coarse = stacked(cfull[...].reshape(SMP, -1))
        for h in range(2):
            high = coarse_high[h * half_rows : (h + 1) * half_rows, :]
            low = coarse_low[h * half_rows : (h + 1) * half_rows, :]
            inner = folded(dot_t(coarse, high)) + dot_t(coarse[:SMP], low)
            ipart[h * 8 : (h + 1) * 8] = inner.reshape(8, 8, half_rows)

        reduce_sub(5 * turn + 2, ipart, irecv, ifull, 64)
        lifted = jnp.zeros((SMP, coarse_v.shape[1]), F32)
        for h in range(2):
            high = coarse_high[h * half_rows : (h + 1) * half_rows, :]
            low = coarse_low[h * half_rows : (h + 1) * half_rows, :]
            inner = stacked(ifull[h * 8 : (h + 1) * 8].reshape(SMP, half_rows))
            lifted = lifted + folded(dot(inner, high)) + dot(inner[:SMP], low)
        lpart[...] = lifted.reshape(lpart.shape)

        reduce_crs(4 * turn + 2, lpart, lrecv, lfull, 96)
        lifted = stacked(lfull[...].reshape(SMP, -1))
        for i in range(0, n_sub, 2):
            back_send[:, i * LIMIT : (i + 2) * LIMIT] = folded(
                dot(lifted, scatter_v[:, i * LIMIT : (i + 2) * LIMIT])
            )

        def back_copy(j):
            return sub_copy(5 * turn + 4, j, lanes(back_send, sub_peer(j)), lanes(back_recv, sub))

        def back_wait(j):
            return sub_copy(5 * turn + 4, j, lanes(back_send, sub_peer(j)), lanes(back_recv, sub_from(j)))

        start_all(n_sub, back_copy)
        back_recv[:, own] = back_send[:, own]
        if turn == 0:
            for copy in cond_copies:
                copy.wait()
            loads[8].wait()

            @pl.loop(0, blocks)
            def _(b):
                at = pl.multiple_of(b * BS, BS)
                cond = cond_v[:, pl.ds(pl.multiple_of(at + halo, BS), BS)]
                up = jnp.where(lane < BS - 1, 0.5 * (cond + pltpu.roll(cond, BS - 1, 1)), 0.0)
                down = jnp.where(lane > 0, 0.5 * (cond + pltpu.roll(cond, 1, 1)), 0.0)
                whole = kappa_ref[:, pl.ds(at, BS)] + up + down
                for k in range(4):
                    other = pl.ds(partner_ref[k * blocks + b] * BS, BS)
                    weight = 0.5 * (cond + cond_v[:, other])
                    rates_v[b, k : k + 1] = weight
                    whole = whole + weight
                rates_v[b, 4:5] = whole
                rates_v[b, 5:6] = up
                rates_v[b, 6:7] = down

        wait_all(n_sub, back_wait)
        slot_v[...] = stacked(folded(dot(stacked(back_recv[...]), place_v[...])))

        def lift(i):
            at = pl.multiple_of(i * chunk, chunk)
            span = pl.ds(at, chunk)
            hot = one_hot(lax.broadcasted_iota(jnp.int32, (slots, chunk), 0) == slot_ref[:, span].astype(jnp.int32))
            inside = pl.ds(pl.multiple_of(at + halo, BS), chunk)
            z = ext_v[:, inside] + weight_ref[:, span] * folded(dot(slot_v[...], hot))
            ext_v[:, inside] = z
            product = z * src_v[:, span]
            total = product[:, :BS]
            for k in range(1, chunk // BS):
                total = total + product[:, k * BS : (k + 1) * BS]
            dots_ref[2 * turn] += total

        @pl.loop(0, 2)
        def _(i):
            lift(i * (chunks - 1))

        halo_now = halo_copies(ext_v, 2 + 2 * turn)
        for copy in halo_now:
            copy.start()

        @pl.loop(1, chunks - 1)
        def _(i):
            lift(i)

        for copy in halo_now:
            copy.wait()

        per_turn = 8

        def operator(g, total):
            images = []
            for i in range(per_turn):
                b = g * per_turn + i
                v = ext_v[:, pl.ds(pl.multiple_of(b * BS + halo, BS), BS)]
                rates = rates_v[b]
                image = rates[4:5] * v
                image = image - rates[5:6] * pltpu.roll(v, BS - 1, 1)
                image = image - rates[6:7] * pltpu.roll(v, 1, 1)
                for k in range(4):
                    other = pl.ds(partner_ref[k * blocks + b] * BS, BS)
                    image = image - rates[k : k + 1] * ext_v[:, other]
                images.append(image)
                total = total + v * image
            for i in range(per_turn):
                at = pl.multiple_of((g * per_turn + i) * BS, BS)
                q_v[:, pl.ds(at, BS)] = images[i]
            return total

        zero = jnp.zeros((SMP, BS), F32)
        if turn == 0:
            groups = wide // BS // per_turn

            def operate(i, total):
                for g in range(groups):
                    total = operator(i * groups + g, total)
                return total

            def both(i, total):
                restrict(q_v, i - 1)
                return operate(i, total)

            acc_v[...] = jnp.zeros_like(acc_v)
            first = operate(0, zero)
            dots_ref[1] = lax.fori_loop(1, nodes // wide, both, first)
            restrict(q_v, nodes // wide - 1)
        else:
            dots_ref[3] = lax.fori_loop(0, blocks // per_turn, operator, zero)

    apply(0, src_v, ext_one, image_one)
    apply(1, image_one, ext_two, image_two)

    kind = lax.broadcasted_iota(jnp.int32, (8, BS), 0)
    packed = jnp.zeros((8, BS), F32)
    ones = jnp.ones((8, BS), F32)
    for i in range(4):
        sums = lax.dot_general(
            ones,
            jnp.concatenate([dots_ref[i], jnp.zeros((BS - SMP, BS), F32)], axis=0),
            (((1,), (1,)), ((), ())),
            precision=lax.Precision.HIGHEST,
            preferred_element_type=F32,
        )
        packed = jnp.where(kind == i, sums, packed)
    sums_mine[...] = packed

    def sums_out(j):
        return crs_copy(8, j, sums_mine, sums_crs.at[crs])

    def sums_come(j):
        return crs_copy(8, j, sums_mine, sums_crs.at[crs_from(j)])

    def part_out(j):
        return sub_copy(10, j, sums_part, sums_sub.at[sub])

    def part_come(j):
        return sub_copy(10, j, sums_part, sums_sub.at[sub_from(j)])

    start_all(n_crs, sums_out)
    sums_crs[crs] = sums_mine[...]
    wait_all(n_crs, sums_come)
    sums_part[...] = jnp.sum(sums_crs[...], axis=0)
    start_all(n_sub, part_out)
    sums_sub[sub] = sums_part[...]
    wait_all(n_sub, part_come)
    sums = jnp.sum(sums_sub[...], axis=0)
    rz, zq, qu, ut = (sums[i : i + 1] for i in range(4))
    step = rz / zq
    rz_next = step * step * qu - rz
    ratio = rz_next / rz
    grown = 1.0 + ratio
    curvature = grown * grown * zq - 2.0 * grown * step * qu + step * step * ut
    step_next = rz_next / curvature
    near = jnp.transpose(jnp.broadcast_to(step + step_next * grown, (BS, BS)))[:SMP]
    far = jnp.transpose(jnp.broadcast_to(step * step_next, (BS, BS)))[:SMP]

    @pl.loop(0, blocks // 2)
    def _(g):
        for k in range(2):
            at = pl.multiple_of((g * 2 + k) * BS, BS)
            span = pl.ds(at, BS)
            inside = pl.ds(pl.multiple_of(at + halo, BS), BS)
            residual = src_v[:, span] - near * image_one[:, span] + far * image_two[:, span]
            image_one[:, span] = near * ext_one[:, inside] - far * ext_two[:, inside]
            image_two[:, span] = residual


def apply_call(n_sub, n_crs, src, factor, coarse_factor, real, name, partner):
    nodes = src.shape[1]
    blocks = factor.shape[0]
    slots = name.shape[1] // 2
    rows, cols = coarse_factor.shape
    halo = HALO * BS
    vmem = pl.BlockSpec(memory_space=pltpu.VMEM)
    anywhere = pl.BlockSpec(memory_space=pltpu.HBM)
    wide = n_sub * LIMIT
    field = jax.ShapeDtypeStruct(src.shape, F32)
    return pl.pallas_call(
        functools.partial(apply_kernel, n_sub, n_crs),
        out_shape=(field, field),
        in_specs=[anywhere] * 5 + [pl.BlockSpec(memory_space=pltpu.SMEM)],
        out_specs=(vmem,) * 2,
        scratch_shapes=[
            pltpu.VMEM((SMP, nodes + 2 * halo), F32),
            pltpu.VMEM((SMP, nodes + 2 * halo), F32),
            pltpu.VMEM((1, nodes), F32),
            pltpu.VMEM((1, nodes), F32),
            pltpu.VMEM((1, nodes), F32),
            pltpu.VMEM((1, slots), jnp.int32),
            pltpu.VMEM((1, slots), jnp.int32),
            pltpu.VMEM((rows, cols), BF16),
            pltpu.VMEM((rows, cols), BF16),
            pltpu.VMEM((SMP, nodes), F32),
            pltpu.VMEM((blocks, BS, BS), F32),
            pltpu.VMEM((rows, cols), F32),
            pltpu.VMEM((1, nodes + 2 * halo), F32),
            pltpu.VMEM((slots, 2 * SMP), F32),
            pltpu.VMEM((wide, slots), BF16),
            pltpu.VMEM((cols, wide), BF16),
            pltpu.VMEM((n_sub, 8, LIMIT), F32),
            pltpu.VMEM((n_sub, 8, LIMIT), F32),
            pltpu.VMEM((SMP, wide), F32),
            pltpu.VMEM((SMP, wide), F32),
            pltpu.VMEM((SMP, wide), F32),
            pltpu.VMEM((SMP, wide), F32),
            pltpu.VMEM((n_crs, 8, cols), F32),
            pltpu.VMEM((n_crs, 8, cols), F32),
            pltpu.VMEM((n_crs, 8, cols), F32),
            pltpu.VMEM((n_sub, 8, rows // 2), F32),
            pltpu.VMEM((n_sub, 8, rows // 2), F32),
            pltpu.VMEM((n_sub, 8, rows // 2), F32),
            pltpu.VMEM((n_crs, 8, cols), F32),
            pltpu.VMEM((n_crs, 8, cols), F32),
            pltpu.VMEM((n_crs, 8, cols), F32),
            pltpu.VMEM((2 * SMP, slots), BF16),
            pltpu.VMEM((blocks, 8, BS), F32),
            pltpu.VMEM((4, SMP, BS), F32),
            pltpu.VMEM((8, BS), F32),
            pltpu.VMEM((n_crs, 8, BS), F32),
            pltpu.VMEM((8, BS), F32),
            pltpu.VMEM((n_sub, 8, BS), F32),
            pltpu.SemaphoreType.DMA((9,)),
            pltpu.SemaphoreType.DMA((11, n_sub)),
            pltpu.SemaphoreType.DMA((11, n_sub)),
            pltpu.SemaphoreType.DMA((9, n_crs)),
            pltpu.SemaphoreType.DMA((9, n_crs)),
            pltpu.SemaphoreType.DMA((6,)),
            pltpu.SemaphoreType.DMA((6,)),
        ],
        compiler_params=pltpu.CompilerParams(
            collective_id=0, has_side_effects=True, vmem_limit_bytes=VMEM_LIMIT * 1024 * 1024
        ),
    )(src, factor, coarse_factor, real, name, partner)


def solution(mesh):
    n_sub, n_crs = mesh.shape["sub"], mesh.shape["crs"]

    def per_device(
        right_side,
        kappa_sq,
        conduct,
        partners,
        local_factor,
        restrict_weight,
        aggregate,
        owner,
        owner_coarse_row,
        coarse_factor,
    ):
        nodes = right_side.shape[1]
        slots = owner.shape[0]
        first_block = lax.axis_index(("sub", "crs")) * local_factor.shape[0] - HALO
        rest = (
            local_factor,
            coarse_factor,
            jnp.concatenate(
                [restrict_weight, kappa_sq, conduct, aggregate[0].astype(F32)]
            ).reshape(1, 4 * nodes),
            jnp.concatenate([owner.reshape(slots), owner_coarse_row]).reshape(1, 2 * slots),
            (partners.T - first_block).reshape(-1),
        )
        return apply_call(n_sub, n_crs, right_side, *rest)

    return jax.shard_map(
        per_device,
        mesh=mesh,
        in_specs=(
            P(None, ("sub", "crs")),
            P(("sub", "crs")),
            P(("sub", "crs")),
            P(("sub", "crs"), None),
            P(("sub", "crs"), None, None),
            P(("sub", "crs")),
            P(("sub", "crs"), None),
            P(("sub", "crs"), None),
            P(("sub", "crs")),
            P("crs", "sub"),
        ),
        out_specs=(P(None, ("sub", "crs")), P(None, ("sub", "crs"))),
        check_vma=False,
    )
```

```python
import functools

import jax
import jax.numpy as jnp
from jax import lax
from jax.experimental import pallas as pl
from jax.experimental.pallas import tpu as pltpu
from jax.sharding import PartitionSpec as P

MESH = pl.DeviceIdType.MESH
F32 = jnp.float32
BF16 = jnp.bfloat16
HALO = 7
BS = 128
SMP = 64
LIMIT = 128
RING = 4
CORES = 2
VMEM_LIMIT = 40


def split(x):
    high = x.astype(BF16)
    return high, (x - high.astype(F32)).astype(BF16)


def dot(a, b):
    return lax.dot_general(a, b, (((1,), (0,)), ((), ())), preferred_element_type=F32)


def dot_t(a, b):
    return lax.dot_general(a, b, (((1,), (1,)), ((), ())), preferred_element_type=F32)


def stacked(x):
    return jnp.concatenate(split(x), axis=0)


def folded(y):
    half = y.shape[0] // 2
    return y[:half] + y[half:]


def farthest_first(count, depth):
    width = count // depth

    def hops(j):
        outer, inner = j // depth, j % depth
        return 2 * min(outer, width - outer) + 2 * min(inner, depth - inner) * (depth > CORES)

    return sorted(range(1, count), key=lambda j: (-hops(j), j))


def one_hot(mask):
    return jnp.where(mask, 1.0, 0.0).astype(BF16)


def apply_kernel(
    n_sub,
    n_crs,
    src_hbm,
    factor_hbm,
    coarse_hbm,
    real_hbm,
    name_hbm,
    partner_ref,
    image_one,
    image_two,
    ext_one,
    ext_two,
    weight_ref,
    kappa_ref,
    slot_ref,
    owner_ref,
    row_ref,
    coarse_high,
    coarse_low,
    src_v,
    factor_v,
    coarse_v,
    cond_v,
    acc_v,
    place_v,
    scatter_v,
    index_send,
    index_recv,
    slot_send,
    slot_recv,
    back_send,
    back_recv,
    cpart,
    crecv,
    cfull,
    ipart,
    irecv,
    ifull,
    lpart,
    lrecv,
    lfull,
    slot_v,
    rates_v,
    dots_ref,
    sums_mine,
    sums_crs,
    sums_part,
    sums_sub,
    load_sem,
    sub_send,
    sub_recv,
    crs_send,
    crs_recv,
    halo_send,
    halo_recv,
):
    sub = lax.axis_index("sub")
    crs = lax.axis_index("crs")
    me = sub * n_crs + crs
    total = n_sub * n_crs
    right = lax.rem(me + 1, total)
    left = lax.rem(me + total - 1, total)
    nodes = src_v.shape[1]
    blocks = nodes // BS
    slots = owner_ref.shape[1]
    halo = HALO * BS

    def shifted(place, j, width, depth, sign):
        outer = lax.rem(lax.div(place, depth) + width + sign * (j // depth), width)
        inner = lax.rem(lax.rem(place, depth) + depth + sign * (j % depth), depth)
        return outer * depth + inner

    def sub_peer(j):
        return shifted(sub, j, n_sub // RING, RING, 1)

    def sub_from(j):
        return shifted(sub, j, n_sub // RING, RING, -1)

    def crs_peer(j):
        return shifted(crs, j, n_crs // CORES, CORES, 1)

    def crs_from(j):
        return shifted(crs, j, n_crs // CORES, CORES, -1)

    def at_device(d):
        return (d // n_crs, lax.rem(d, n_crs))

    def sub_copy(phase, j, source, target):
        return pltpu.make_async_remote_copy(
            src_ref=source,
            dst_ref=target,
            send_sem=sub_send.at[phase, j],
            recv_sem=sub_recv.at[phase, j],
            device_id=(sub_peer(j), crs),
            device_id_type=MESH,
        )

    def crs_copy(phase, j, source, target):
        return pltpu.make_async_remote_copy(
            src_ref=source,
            dst_ref=target,
            send_sem=crs_send.at[phase, j],
            recv_sem=crs_recv.at[phase, j],
            device_id=(sub, crs_peer(j)),
            device_id_type=MESH,
        )

    def lanes(ref, i):
        return ref.at[:, pl.ds(pl.multiple_of(i * LIMIT, LIMIT), LIMIT)]

    def start_all(count, copy):
        for j in farthest_first(count, RING if count == n_sub else CORES):
            copy(j).start()

    def wait_all(count, copy):
        @pl.loop(1, count)
        def _(j):
            copy(j).wait()

    loads = [
        pltpu.make_async_copy(src_hbm, src_v, load_sem.at[0]),
        pltpu.make_async_copy(factor_hbm, factor_v, load_sem.at[1]),
        pltpu.make_async_copy(coarse_hbm, coarse_v, load_sem.at[2]),
        pltpu.make_async_copy(real_hbm.at[:, pl.ds(0, nodes)], weight_ref, load_sem.at[3]),
        pltpu.make_async_copy(real_hbm.at[:, pl.ds(3 * nodes, nodes)], slot_ref, load_sem.at[4]),
        pltpu.make_async_copy(name_hbm.at[:, pl.ds(0, slots)], owner_ref, load_sem.at[5]),
        pltpu.make_async_copy(name_hbm.at[:, pl.ds(slots, slots)], row_ref, load_sem.at[6]),
        pltpu.make_async_copy(
            real_hbm.at[:, pl.ds(2 * nodes, nodes)],
            cond_v.at[:, pl.ds(halo, nodes)],
            load_sem.at[7],
        ),
        pltpu.make_async_copy(real_hbm.at[:, pl.ds(nodes, nodes)], kappa_ref, load_sem.at[8]),
    ]
    for i in (5, 6, 7, 3, 4, 0, 8, 1, 2):
        loads[i].start()

    barrier = pltpu.get_barrier_semaphore()

    @pl.loop(1, n_sub)
    def _(j):
        pl.semaphore_signal(barrier, inc=1, device_id=(sub_peer(j), crs), device_id_type=MESH)

    @pl.loop(1, n_crs)
    def _(j):
        pl.semaphore_signal(barrier, inc=1, device_id=(sub, crs_peer(j)), device_id_type=MESH)

    pl.semaphore_signal(barrier, inc=1, device_id=at_device(left), device_id_type=MESH)
    pl.semaphore_signal(barrier, inc=1, device_id=at_device(right), device_id_type=MESH)

    loads[5].wait()
    loads[6].wait()
    owner_row = owner_ref[...]
    group = lax.broadcasted_iota(jnp.int32, (n_sub, slots), 0)
    members = jnp.where(owner_row == group, 1.0, 0.0)
    before = one_hot(
        lax.broadcasted_iota(jnp.int32, (slots, slots), 0)
        < lax.broadcasted_iota(jnp.int32, (slots, slots), 1)
    )
    ahead = dot(members.astype(BF16), before)
    rank = jnp.sum(members * ahead, axis=0, keepdims=True)
    place = owner_row * LIMIT + rank.astype(jnp.int32)
    row_one = stacked(jnp.broadcast_to((row_ref[...] + 1).astype(F32), (8, slots)))

    wide = 2048
    lists = n_sub * wide // nodes

    def list_slots(i):
        start = pl.multiple_of(i * lists * LIMIT, lists * LIMIT)
        hot = one_hot(
            lax.broadcasted_iota(jnp.int32, (lists * LIMIT, slots), 0) + start == place
        )
        place_v[pl.ds(start, lists * LIMIT), :] = hot
        index = folded(dot_t(row_one, hot)) - 1.0
        for k in range(lists):
            index_send[i * lists + k] = index[:, k * LIMIT : (k + 1) * LIMIT]

    def index_copy(j):
        return sub_copy(0, j, index_send.at[sub_peer(j)], index_recv.at[sub])

    def index_wait(j):
        return sub_copy(0, j, index_send.at[sub_peer(j)], index_recv.at[sub_from(j)])

    def halo_copies(buffer, phase):
        up = pltpu.make_async_remote_copy(
            src_ref=buffer.at[:, pl.ds(nodes, halo)],
            dst_ref=buffer.at[:, pl.ds(0, halo)],
            send_sem=halo_send.at[phase],
            recv_sem=halo_recv.at[phase],
            device_id=at_device(right),
            device_id_type=MESH,
        )
        down = pltpu.make_async_remote_copy(
            src_ref=buffer.at[:, pl.ds(halo, halo)],
            dst_ref=buffer.at[:, pl.ds(halo + nodes, halo)],
            send_sem=halo_send.at[phase + 1],
            recv_sem=halo_recv.at[phase + 1],
            device_id=at_device(left),
            device_id_type=MESH,
        )
        return up, down

    cond_copies = halo_copies(cond_v, 0)

    half_rows = coarse_v.shape[0] // 2
    own = pl.ds(pl.multiple_of(sub * LIMIT, LIMIT), LIMIT)
    chunk = 1024
    chunks = nodes // chunk
    lane = lax.broadcasted_iota(jnp.int32, (1, BS), 1)
    dots_ref[...] = jnp.zeros_like(dots_ref)

    def restrict(values, i):
        span = pl.ds(pl.multiple_of(i * wide, wide), wide)
        weighted = stacked(values[:, span] * weight_ref[:, span])
        hot = one_hot(lax.broadcasted_iota(jnp.int32, (slots, wide), 0) == slot_ref[:, span].astype(jnp.int32))
        acc_v[...] += dot_t(hot, weighted)

    def apply(turn, src_v, ext_v, q_v):
        if turn == 0:
            loads[3].wait()
            loads[4].wait()
            loads[0].wait()
        if turn == 0:
            acc_v[...] = jnp.zeros_like(acc_v)

            @pl.loop(0, nodes // wide)
            def _(i):
                restrict(src_v, i)
                list_slots(i)

            index_recv[sub] = index_send[sub]
            loads[7].wait()
            pl.semaphore_wait(barrier, n_sub + n_crs)
            start_all(n_sub, index_copy)

        tiles = stacked(folded(jnp.transpose(acc_v[...])))
        for i in range(0, n_sub, 2):
            slot_send[:, i * LIMIT : (i + 2) * LIMIT] = folded(
                dot_t(tiles, place_v[i * LIMIT : (i + 2) * LIMIT, :])
            )

        def slot_copy(j):
            return sub_copy(5 * turn + 1, j, lanes(slot_send, sub_peer(j)), lanes(slot_recv, sub))

        def slot_wait(j):
            return sub_copy(5 * turn + 1, j, lanes(slot_send, sub_peer(j)), lanes(slot_recv, sub_from(j)))

        start_all(n_sub, slot_copy)
        if turn == 0:
            for copy in cond_copies:
                copy.start()
        slot_recv[:, own] = slot_send[:, own]

        def local(first, last):
            @pl.loop(first // 4, last // 4)
            def _(g):
                for k in range(4):
                    b = g * 4 + k
                    at = pl.multiple_of(b * BS, BS)
                    values = stacked(src_v[:, pl.ds(at, BS)])
                    high, low = split(factor_v[b])
                    half = folded(dot(values, high)) + dot(values[:SMP], low)
                    half = stacked(half)
                    ext_v[:, pl.ds(pl.multiple_of(at + halo, BS), BS)] = folded(
                        dot_t(half, high)
                    ) + dot_t(half[:SMP], low)

        if turn == 0:
            loads[1].wait()
        local(0, 16)

        if turn == 0:
            wait_all(n_sub, index_wait)

            @pl.loop(0, n_sub)
            def _(i):
                index = index_recv[i][0:1, :].astype(jnp.int32)
                rows = scatter_v.shape[0]
                span = pl.ds(pl.multiple_of(i * LIMIT, LIMIT), LIMIT)
                scatter_v[:, span] = one_hot(lax.broadcasted_iota(jnp.int32, (rows, LIMIT), 0) == index)

        if turn == 0:
            loads[2].wait()
            step_rows = 128

            @pl.loop(0, coarse_v.shape[0] // step_rows)
            def _(i):
                span = pl.ds(pl.multiple_of(i * step_rows, step_rows), step_rows)
                high, low = split(coarse_v[span, :])
                coarse_high[span, :] = high
                coarse_low[span, :] = low

        wait_all(n_sub, slot_wait)
        coarse_part = folded(dot_t(stacked(slot_recv[...]), scatter_v[...]))
        cpart[...] = coarse_part.reshape(cpart.shape)

        def reduce_sub(phase, part, recv, full, gap):
            def out(j):
                return sub_copy(phase, j, part.at[sub_peer(j)], recv.at[sub])

            def come(j):
                return sub_copy(phase, j, part.at[sub_peer(j)], recv.at[sub_from(j)])

            def share(j):
                return sub_copy(phase + 1, j, full.at[sub], full.at[sub])

            def shared(j):
                return sub_copy(phase + 1, j, full.at[sub], full.at[sub_from(j)])

            start_all(n_sub, out)
            recv[sub] = part[sub]
            local(gap, gap + 24)
            wait_all(n_sub, come)
            full[sub] = jnp.sum(recv[...], axis=0)
            start_all(n_sub, share)
            local(gap + 24, gap + 48)
            wait_all(n_sub, shared)

        def reduce_crs(phase, part, recv, full, gap):
            def out(j):
                return crs_copy(phase, j, part.at[crs_peer(j)], recv.at[crs])

            def come(j):
                return crs_copy(phase, j, part.at[crs_peer(j)], recv.at[crs_from(j)])

            def share(j):
                return crs_copy(phase + 1, j, full.at[crs], full.at[crs])

            def shared(j):
                return crs_copy(phase + 1, j, full.at[crs], full.at[crs_from(j)])

            start_all(n_crs, out)
            recv[crs] = part[crs]
            local(gap, gap + 16)
            wait_all(n_crs, come)
            full[crs] = jnp.sum(recv[...], axis=0)
            start_all(n_crs, share)
            local(gap + 16, gap + 32)
            wait_all(n_crs, shared)

        reduce_crs(4 * turn, cpart, crecv, cfull, 16)
        coarse = stacked(cfull[...].reshape(SMP, -1))
        for h in range(2):
            high = coarse_high[h * half_rows : (h + 1) * half_rows, :]
            low = coarse_low[h * half_rows : (h + 1) * half_rows, :]
            inner = folded(dot_t(coarse, high)) + dot_t(coarse[:SMP], low)
            ipart[h * 8 : (h + 1) * 8] = inner.reshape(8, 8, half_rows)

        reduce_sub(5 * turn + 2, ipart, irecv, ifull, 48)
        lifted = jnp.zeros((SMP, coarse_v.shape[1]), F32)
        for h in range(2):
            high = coarse_high[h * half_rows : (h + 1) * half_rows, :]
            low = coarse_low[h * half_rows : (h + 1) * half_rows, :]
            inner = stacked(ifull[h * 8 : (h + 1) * 8].reshape(SMP, half_rows))
            lifted = lifted + folded(dot(inner, high)) + dot(inner[:SMP], low)
        lpart[...] = lifted.reshape(lpart.shape)

        reduce_crs(4 * turn + 2, lpart, lrecv, lfull, 96)
        lifted = stacked(lfull[...].reshape(SMP, -1))
        for i in range(0, n_sub, 2):
            back_send[:, i * LIMIT : (i + 2) * LIMIT] = folded(
                dot(lifted, scatter_v[:, i * LIMIT : (i + 2) * LIMIT])
            )

        def back_copy(j):
            return sub_copy(5 * turn + 4, j, lanes(back_send, sub_peer(j)), lanes(back_recv, sub))

        def back_wait(j):
            return sub_copy(5 * turn + 4, j, lanes(back_send, sub_peer(j)), lanes(back_recv, sub_from(j)))

        start_all(n_sub, back_copy)
        back_recv[:, own] = back_send[:, own]
        if turn == 0:
            for copy in cond_copies:
                copy.wait()
            loads[8].wait()

            @pl.loop(0, blocks)
            def _(b):
                at = pl.multiple_of(b * BS, BS)
                cond = cond_v[:, pl.ds(pl.multiple_of(at + halo, BS), BS)]
                up = jnp.where(lane < BS - 1, 0.5 * (cond + pltpu.roll(cond, BS - 1, 1)), 0.0)
                down = jnp.where(lane > 0, 0.5 * (cond + pltpu.roll(cond, 1, 1)), 0.0)
                whole = kappa_ref[:, pl.ds(at, BS)] + up + down
                for k in range(4):
                    other = pl.ds(partner_ref[k * blocks + b] * BS, BS)
                    weight = 0.5 * (cond + cond_v[:, other])
                    rates_v[b, k : k + 1] = weight
                    whole = whole + weight
                rates_v[b, 4:5] = whole
                rates_v[b, 5:6] = up
                rates_v[b, 6:7] = down

        wait_all(n_sub, back_wait)
        slot_v[...] = stacked(folded(dot(stacked(back_recv[...]), place_v[...])))

        def lift(i):
            at = pl.multiple_of(i * chunk, chunk)
            span = pl.ds(at, chunk)
            hot = one_hot(lax.broadcasted_iota(jnp.int32, (slots, chunk), 0) == slot_ref[:, span].astype(jnp.int32))
            inside = pl.ds(pl.multiple_of(at + halo, BS), chunk)
            z = ext_v[:, inside] + weight_ref[:, span] * folded(dot(slot_v[...], hot))
            ext_v[:, inside] = z
            product = z * src_v[:, span]
            total = product[:, :BS]
            for k in range(1, chunk // BS):
                total = total + product[:, k * BS : (k + 1) * BS]
            dots_ref[2 * turn] += total

        @pl.loop(0, 2)
        def _(i):
            lift(i * (chunks - 1))

        halo_now = halo_copies(ext_v, 2 + 2 * turn)
        for copy in halo_now:
            copy.start()

        @pl.loop(1, chunks - 1)
        def _(i):
            lift(i)

        for copy in halo_now:
            copy.wait()

        per_turn = 8

        def operator(g, total):
            images = []
            for i in range(per_turn):
                b = g * per_turn + i
                v = ext_v[:, pl.ds(pl.multiple_of(b * BS + halo, BS), BS)]
                rates = rates_v[b]
                image = rates[4:5] * v
                image = image - rates[5:6] * pltpu.roll(v, BS - 1, 1)
                image = image - rates[6:7] * pltpu.roll(v, 1, 1)
                for k in range(4):
                    other = pl.ds(partner_ref[k * blocks + b] * BS, BS)
                    image = image - rates[k : k + 1] * ext_v[:, other]
                images.append(image)
                total = total + v * image
            for i in range(per_turn):
                at = pl.multiple_of((g * per_turn + i) * BS, BS)
                q_v[:, pl.ds(at, BS)] = images[i]
            return total

        zero = jnp.zeros((SMP, BS), F32)
        if turn == 0:
            groups = wide // BS // per_turn

            def operate(i, total):
                for g in range(groups):
                    total = operator(i * groups + g, total)
                return total

            def both(i, total):
                restrict(q_v, i - 1)
                return operate(i, total)

            acc_v[...] = jnp.zeros_like(acc_v)
            first = operate(0, zero)
            dots_ref[1] = lax.fori_loop(1, nodes // wide, both, first)
            restrict(q_v, nodes // wide - 1)
        else:
            dots_ref[3] = lax.fori_loop(0, blocks // per_turn, operator, zero)

    apply(0, src_v, ext_one, image_one)
    apply(1, image_one, ext_two, image_two)

    kind = lax.broadcasted_iota(jnp.int32, (8, BS), 0)
    packed = jnp.zeros((8, BS), F32)
    ones = jnp.ones((8, BS), F32)
    for i in range(4):
        sums = lax.dot_general(
            ones,
            jnp.concatenate([dots_ref[i], jnp.zeros((BS - SMP, BS), F32)], axis=0),
            (((1,), (1,)), ((), ())),
            precision=lax.Precision.HIGHEST,
            preferred_element_type=F32,
        )
        packed = jnp.where(kind == i, sums, packed)
    sums_mine[...] = packed

    def sums_out(j):
        return crs_copy(8, j, sums_mine, sums_crs.at[crs])

    def sums_come(j):
        return crs_copy(8, j, sums_mine, sums_crs.at[crs_from(j)])

    def part_out(j):
        return sub_copy(10, j, sums_part, sums_sub.at[sub])

    def part_come(j):
        return sub_copy(10, j, sums_part, sums_sub.at[sub_from(j)])

    start_all(n_crs, sums_out)
    sums_crs[crs] = sums_mine[...]
    wait_all(n_crs, sums_come)
    sums_part[...] = jnp.sum(sums_crs[...], axis=0)
    start_all(n_sub, part_out)
    sums_sub[sub] = sums_part[...]
    wait_all(n_sub, part_come)
    sums = jnp.sum(sums_sub[...], axis=0)
    rz, zq, qu, ut = (sums[i : i + 1] for i in range(4))
    step = rz / zq
    rz_next = step * step * qu - rz
    ratio = rz_next / rz
    grown = 1.0 + ratio
    curvature = grown * grown * zq - 2.0 * grown * step * qu + step * step * ut
    step_next = rz_next / curvature
    near = jnp.transpose(jnp.broadcast_to(step + step_next * grown, (BS, BS)))[:SMP]
    far = jnp.transpose(jnp.broadcast_to(step * step_next, (BS, BS)))[:SMP]

    @pl.loop(0, blocks // 2)
    def _(g):
        for k in range(2):
            at = pl.multiple_of((g * 2 + k) * BS, BS)
            span = pl.ds(at, BS)
            inside = pl.ds(pl.multiple_of(at + halo, BS), BS)
            residual = src_v[:, span] - near * image_one[:, span] + far * image_two[:, span]
            image_one[:, span] = near * ext_one[:, inside] - far * ext_two[:, inside]
            image_two[:, span] = residual


def apply_call(n_sub, n_crs, src, factor, coarse_factor, real, name, partner):
    nodes = src.shape[1]
    blocks = factor.shape[0]
    slots = name.shape[1] // 2
    rows, cols = coarse_factor.shape
    halo = HALO * BS
    vmem = pl.BlockSpec(memory_space=pltpu.VMEM)
    anywhere = pl.BlockSpec(memory_space=pltpu.HBM)
    wide = n_sub * LIMIT
    field = jax.ShapeDtypeStruct(src.shape, F32)
    return pl.pallas_call(
        functools.partial(apply_kernel, n_sub, n_crs),
        out_shape=(field, field),
        in_specs=[anywhere] * 5 + [pl.BlockSpec(memory_space=pltpu.SMEM)],
        out_specs=(vmem,) * 2,
        scratch_shapes=[
            pltpu.VMEM((SMP, nodes + 2 * halo), F32),
            pltpu.VMEM((SMP, nodes + 2 * halo), F32),
            pltpu.VMEM((1, nodes), F32),
            pltpu.VMEM((1, nodes), F32),
            pltpu.VMEM((1, nodes), F32),
            pltpu.VMEM((1, slots), jnp.int32),
            pltpu.VMEM((1, slots), jnp.int32),
            pltpu.VMEM((rows, cols), BF16),
            pltpu.VMEM((rows, cols), BF16),
            pltpu.VMEM((SMP, nodes), F32),
            pltpu.VMEM((blocks, BS, BS), F32),
            pltpu.VMEM((rows, cols), F32),
            pltpu.VMEM((1, nodes + 2 * halo), F32),
            pltpu.VMEM((slots, 2 * SMP), F32),
            pltpu.VMEM((wide, slots), BF16),
            pltpu.VMEM((cols, wide), BF16),
            pltpu.VMEM((n_sub, 8, LIMIT), F32),
            pltpu.VMEM((n_sub, 8, LIMIT), F32),
            pltpu.VMEM((SMP, wide), F32),
            pltpu.VMEM((SMP, wide), F32),
            pltpu.VMEM((SMP, wide), F32),
            pltpu.VMEM((SMP, wide), F32),
            pltpu.VMEM((n_crs, 8, cols), F32),
            pltpu.VMEM((n_crs, 8, cols), F32),
            pltpu.VMEM((n_crs, 8, cols), F32),
            pltpu.VMEM((n_sub, 8, rows // 2), F32),
            pltpu.VMEM((n_sub, 8, rows // 2), F32),
            pltpu.VMEM((n_sub, 8, rows // 2), F32),
            pltpu.VMEM((n_crs, 8, cols), F32),
            pltpu.VMEM((n_crs, 8, cols), F32),
            pltpu.VMEM((n_crs, 8, cols), F32),
            pltpu.VMEM((2 * SMP, slots), BF16),
            pltpu.VMEM((blocks, 8, BS), F32),
            pltpu.VMEM((4, SMP, BS), F32),
            pltpu.VMEM((8, BS), F32),
            pltpu.VMEM((n_crs, 8, BS), F32),
            pltpu.VMEM((8, BS), F32),
            pltpu.VMEM((n_sub, 8, BS), F32),
            pltpu.SemaphoreType.DMA((9,)),
            pltpu.SemaphoreType.DMA((11, n_sub)),
            pltpu.SemaphoreType.DMA((11, n_sub)),
            pltpu.SemaphoreType.DMA((9, n_crs)),
            pltpu.SemaphoreType.DMA((9, n_crs)),
            pltpu.SemaphoreType.DMA((6,)),
            pltpu.SemaphoreType.DMA((6,)),
        ],
        compiler_params=pltpu.CompilerParams(
            collective_id=0, has_side_effects=True, vmem_limit_bytes=VMEM_LIMIT * 1024 * 1024
        ),
    )(src, factor, coarse_factor, real, name, partner)


def solution(mesh):
    n_sub, n_crs = mesh.shape["sub"], mesh.shape["crs"]

    def per_device(
        right_side,
        kappa_sq,
        conduct,
        partners,
        local_factor,
        restrict_weight,
        aggregate,
        owner,
        owner_coarse_row,
        coarse_factor,
    ):
        nodes = right_side.shape[1]
        slots = owner.shape[0]
        first_block = lax.axis_index(("sub", "crs")) * local_factor.shape[0] - HALO
        rest = (
            local_factor,
            coarse_factor,
            jnp.concatenate(
                [restrict_weight, kappa_sq, conduct, aggregate[0].astype(F32)]
            ).reshape(1, 4 * nodes),
            jnp.concatenate([owner.reshape(slots), owner_coarse_row]).reshape(1, 2 * slots),
            (partners.T - first_block).reshape(-1),
        )
        return apply_call(n_sub, n_crs, right_side, *rest)

    return jax.shard_map(
        per_device,
        mesh=mesh,
        in_specs=(
            P(None, ("sub", "crs")),
            P(("sub", "crs")),
            P(("sub", "crs")),
            P(("sub", "crs"), None),
            P(("sub", "crs"), None, None),
            P(("sub", "crs")),
            P(("sub", "crs"), None),
            P(("sub", "crs"), None),
            P(("sub", "crs")),
            P("crs", "sub"),
        ),
        out_specs=(P(None, ("sub", "crs")), P(None, ("sub", "crs"))),
        check_vma=False,
    )
```
